256 devices in a mesh: len: 64 (over z, x, core), hgt: 4 (over y).
Axes of the slice: x: 4, y: 4, z: 8, core: 2. Of those that a mesh axis runs over, the one named last changes fastest.
Arguments:
- slave_disp: bfloat16 [256, 16, 96, 256], P('len', 'hgt'), may hold values from -6 to 6
- master_disp: bfloat16 [256, 16, 96, 256], P('len', 'hgt'), may hold values from -6 to 6
- quad_coords: float32 [64, 4, 64, 4, 256], P('len', 'hgt'), may hold values from 0 to 1
- quad_weights: float32 [64, 4, 64, 256], P('len', 'hgt'), may hold values from 0.0005 to 0.02
- pair_count: int32 [64, 4], P('len', 'hgt'), may hold values from 24 to 64, as said below
- slave_face: int32 [64, 4, 64], P('len', 'hgt'), may hold values from 0 to 15
- master_row: int32 [64, 4, 64], P('len', 'hgt'), may hold values from 0 to 255, as said below
- master_col: int32 [64, 4, 64], P('len', 'hgt'), may hold values from 0 to 15, as said below
- active: int32 [64, 4, 64], P('len', 'hgt'), may hold values 0 or 1
Outputs:
- master_force: float32 [256, 16, 96, 256], P('len', 'hgt')
- slave_multiplier: float32 [256, 16, 96, 256], P('len', 'hgt')
The draws below stay inside these ranges and needn't reach their ends.
Inputs may be any that keep to these rules, and one draw needn't show every extreme that they name: `pair_count`: some band cell has all 64 slots live in count in every draw; every other cell has between 24 and 56. `master_row`: A pair's master face lies in its own band cell's block of 4 rows or in the block beside it along the length, within the grid. `master_col`: A pair's master face lies in its own band cell's block of 4 columns or in the block beside it along the height, within the grid.
All inputs are finite; a program needn't handle non-finite values. No bound on the sum of `active` on one device may be relied on, other than what follows from the above.
Results may differ from the reference program's by a relative error of at most 0.002.
Values may be sent and summed in bfloat16 or wider, within the bound.
A program may use at most 128 MiB of HBM per device.

```python
import math
import jax
import jax.numpy as jnp
from jax import lax

ORDER = 16
NODES = 256
QUAD = 256
CHANNELS = 96
FACE_SIDE = 4
PAIR_CAP = 64
PAIR_BLOCK = 32
LEN_BANDS = 64
HGT_BANDS = 4
ROWS = 256
HGT_FACES = 16


def draw_pair_count(key, part):
    key_base, key_top = jax.random.split(key)
    cells = LEN_BANDS * HGT_BANDS
    base_counts = jax.random.randint(key_base, (cells,), 3 * PAIR_CAP // 8, 7 * PAIR_CAP // 8 + 1)
    busiest = jax.random.randint(key_top, (), 0, cells)
    filled = jnp.where(jnp.arange(cells) == busiest, PAIR_CAP, base_counts)
    return filled.reshape(LEN_BANDS, HGT_BANDS).astype(jnp.int32)


def draw_master_row(key, part):
    band_len = jnp.arange(LEN_BANDS, dtype=jnp.int32)[:, None, None]
    lowest = jnp.maximum(0, (band_len - 1) * FACE_SIDE)
    highest = jnp.minimum(ROWS, (band_len + 2) * FACE_SIDE)
    lowest = jnp.broadcast_to(lowest, (LEN_BANDS, HGT_BANDS, PAIR_CAP))
    highest = jnp.broadcast_to(highest, (LEN_BANDS, HGT_BANDS, PAIR_CAP))
    return jax.random.randint(key, (LEN_BANDS, HGT_BANDS, PAIR_CAP), lowest, highest).astype(jnp.int32)


def draw_master_col(key, part):
    band_hgt = jnp.arange(HGT_BANDS, dtype=jnp.int32)[None, :, None]
    lowest = jnp.maximum(0, (band_hgt - 1) * FACE_SIDE)
    highest = jnp.minimum(HGT_FACES, (band_hgt + 2) * FACE_SIDE)
    lowest = jnp.broadcast_to(lowest, (LEN_BANDS, HGT_BANDS, PAIR_CAP))
    highest = jnp.broadcast_to(highest, (LEN_BANDS, HGT_BANDS, PAIR_CAP))
    return jax.random.randint(jax.random.fold_in(key, 7), (LEN_BANDS, HGT_BANDS, PAIR_CAP), lowest, highest).astype(jnp.int32)


def place_ends(drawn, key, low, top_value):
    longest = drawn.shape.index(max(drawn.shape))
    spots = []
    for shift in (0, 1):
        where = [jax.random.randint(jax.random.fold_in(key, axis), (), 0, length) for axis, length in enumerate(drawn.shape)]
        where[longest] = (where[longest] + shift) % drawn.shape[longest]
        spots.append(tuple(where))
    return drawn.at[spots[0]].set(low).at[spots[1]].set(top_value)


def block_levels(stream_key, extent, cuts, smallest, high):
    factor_of, own = 1.0, jax.random.fold_in(stream_key, 6)
    for position, parts in cuts:
        steps = jnp.exp(jax.random.uniform(jax.random.fold_in(own, position), (parts,), jnp.float32, smallest / len(cuts), high / len(cuts)))
        factor_of = factor_of * jnp.repeat(steps, extent[position] // parts).reshape([-1 if axis == position else 1 for axis in range(len(extent))])
    return factor_of


def normal_values(rng, extent, width, bound, cuts=(), kind=jnp.bfloat16):
    level = block_levels(rng, extent, cuts, -0.22, 0.18) if cuts else 1.0
    array = jax.random.normal(rng, extent, jnp.float32) * width * level
    return jnp.minimum(jnp.maximum(array, -bound), bound).astype(kind)


def setup_inputs(seed: int = 0) -> dict:
    key_of = jax.random.split(jax.random.key(seed), 10)
    slave_disp = normal_values(key_of[0], (ROWS, HGT_FACES, CHANNELS, NODES), 1.0, 6.0, ((0, 64), (1, 4)))
    master_disp = normal_values(key_of[1], (ROWS, HGT_FACES, CHANNELS, NODES), 1.0, 6.0, ((0, 64), (1, 4)))
    quad_coords = jnp.clip(1.0 * jax.random.uniform(key_of[2], (LEN_BANDS, HGT_BANDS, PAIR_CAP, 4, QUAD), jnp.float32) ** block_levels(key_of[2], (LEN_BANDS, HGT_BANDS, PAIR_CAP, 4, QUAD), ((0, 64), (1, 4)), -0.2, 0.2), 0.0, 1.0)
    quad_weights = jnp.clip(jnp.exp(math.log(0.02) - 3.6888794 * jax.random.uniform(key_of[3], (LEN_BANDS, HGT_BANDS, PAIR_CAP, QUAD), jnp.float32) ** block_levels(key_of[3], (LEN_BANDS, HGT_BANDS, PAIR_CAP, QUAD), ((0, 64), (1, 4)), -0.2, 0.2)), 0.0005, 0.02)
    pair_count = draw_pair_count(jax.random.fold_in(key_of[9], 71), 0)
    slave_face = place_ends(jax.random.randint(key_of[5], (LEN_BANDS, HGT_BANDS, PAIR_CAP), 0, FACE_SIDE * FACE_SIDE), jax.random.fold_in(key_of[5], 1), 0, (FACE_SIDE * FACE_SIDE) - 1).astype(jnp.int32)
    master_row = draw_master_row(jax.random.fold_in(key_of[9], 71), 0)
    master_col = draw_master_col(jax.random.fold_in(key_of[9], 71), 0)
    active = place_ends((jax.random.randint(key_of[8], (LEN_BANDS, HGT_BANDS, PAIR_CAP), 0, 4) < 3).astype(jnp.int32), jax.random.fold_in(key_of[8], 1), 0, 1)
    return dict(slave_disp=slave_disp, master_disp=master_disp, quad_coords=quad_coords, quad_weights=quad_weights, pair_count=pair_count, slave_face=slave_face, master_row=master_row, master_col=master_col, active=active)


def face_basis(points, basis_order):
    mode_numbers = jnp.arange(basis_order, dtype=jnp.float32)
    return jnp.cos(jnp.pi * mode_numbers[None, :, None] * points[:, None, :])


def coupling(coords_block, weights_block, basis_order):
    pairs = coords_block.shape[0]
    quad_pts = coords_block.shape[2]
    slave_first = face_basis(coords_block[:, 0], basis_order)
    slave_second = face_basis(coords_block[:, 1], basis_order)
    master_first = face_basis(coords_block[:, 2], basis_order)
    master_second = face_basis(coords_block[:, 3], basis_order)
    slave_table = (slave_first[:, :, None, :] * slave_second[:, None, :, :]).reshape(pairs, basis_order * basis_order, quad_pts)
    master_table = (master_first[:, :, None, :] * master_second[:, None, :, :]).reshape(pairs, basis_order * basis_order, quad_pts)
    mortar = jnp.einsum("pjq,pkq->pjk", slave_table, master_table * weights_block[:, None, :], precision=lax.Precision.HIGHEST)
    dual_diag = jnp.sum(weights_block[:, None, :] * slave_table * slave_table, axis=2)
    return mortar.astype(jnp.bfloat16), dual_diag


def reference(slave_disp, master_disp, quad_coords, quad_weights, pair_count, slave_face, master_row, master_col, active):
    total = LEN_BANDS * HGT_BANDS * PAIR_CAP
    slot_ids = jnp.arange(total, dtype=jnp.int32)
    cell_ids = slot_ids // PAIR_CAP
    band_len = cell_ids // HGT_BANDS
    band_hgt = cell_ids % HGT_BANDS
    slot_in = slot_ids % PAIR_CAP
    counts = pair_count.reshape(-1)[cell_ids]
    live = ((slot_in < counts) & (active.reshape(-1) == 1)).astype(jnp.float32)
    local_face = slave_face.reshape(-1)
    slave_index = ((band_len * FACE_SIDE + local_face // FACE_SIDE) * HGT_FACES + band_hgt * FACE_SIDE + local_face % FACE_SIDE).astype(jnp.int32)
    master_index = (master_row.reshape(-1) * HGT_FACES + master_col.reshape(-1)).astype(jnp.int32)
    slave_rows = slave_disp.reshape(ROWS * HGT_FACES, CHANNELS, NODES)
    master_rows = master_disp.reshape(ROWS * HGT_FACES, CHANNELS, NODES)
    coords_all = quad_coords.reshape(total, 4, QUAD)
    weights_all = quad_weights.reshape(total, QUAD)
    blocks = total // PAIR_BLOCK

    def visit(totals, block_index):
        first_slot = block_index * PAIR_BLOCK
        live_block = lax.dynamic_slice_in_dim(live, first_slot, PAIR_BLOCK, 0)

        def work(state):
            forces, slave_sum = state
            coords_block = lax.dynamic_slice_in_dim(coords_all, first_slot, PAIR_BLOCK, 0)
            weights_block = lax.dynamic_slice_in_dim(weights_all, first_slot, PAIR_BLOCK, 0)
            sidx = lax.dynamic_slice_in_dim(slave_index, first_slot, PAIR_BLOCK, 0)
            midx = lax.dynamic_slice_in_dim(master_index, first_slot, PAIR_BLOCK, 0)
            mortar, dual_diag = coupling(coords_block, weights_block, ORDER)
            slave_part = slave_rows[sidx].astype(jnp.float32)
            master_part = master_rows[midx].astype(jnp.float32)
            projected = jnp.einsum("pck,pjk->pcj", master_part, mortar.astype(jnp.float32))
            weighted_gap = slave_part * dual_diag[:, None, :] - projected
            multiplier = live_block[:, None, None] * weighted_gap / dual_diag[:, None, :]
            multiplier_b = multiplier.astype(jnp.bfloat16)
            push = jnp.einsum("pcj,pjk->pck", multiplier_b.astype(jnp.float32), mortar.astype(jnp.float32))
            return (forces.at[midx].add(push), slave_sum.at[sidx].add(multiplier))

        return lax.cond(jnp.sum(live_block) > 0.0, work, lambda state: state, totals), None

    start_totals = (jnp.zeros((ROWS * HGT_FACES, CHANNELS, NODES), jnp.float32), jnp.zeros((ROWS * HGT_FACES, CHANNELS, NODES), jnp.float32))
    (forces, slave_sum), _ = lax.scan(visit, start_totals, jnp.arange(blocks, dtype=jnp.int32))
    return (forces.reshape(ROWS, HGT_FACES, CHANNELS, NODES), slave_sum.reshape(ROWS, HGT_FACES, CHANNELS, NODES))
```

```python
import functools

import jax
import jax.numpy as jnp
from jax import lax
from jax.experimental import pallas as pl
from jax.experimental.pallas import tpu as pltpu
from jax.sharding import PartitionSpec as P

ORDER = 16
NODES = 256
CHANNELS = 96
FACES = 16
PAIRS = 64
GROUP = 16
LOCK_A = 4
LOCK_B = 8
CHUNKS = 4
PART = FACES // CHUNKS
EXTRA = 1
F32, BF16 = jnp.float32, jnp.bfloat16
MESH = pl.DeviceIdType.MESH
NT = (((1,), (1,)), ((), ()))
NN = (((1,), (0,)), ((), ()))

OWN, PARTNER, OTHER = range(3)
DOWN, UP, MID = range(3)
BLOCKS = 9
SPOTS = BLOCKS * FACES

AT_PAIR, AT_MASTER, AT_SLAVE, AT_LIVE, AT_KEEP = (i * PAIRS for i in range(5))
AT_LAST = 5 * PAIRS
AT_HAS = AT_LAST + SPOTS


def cos_pi(turns):
    reduced = turns - 2.0 * jnp.round(turns * 0.5)
    s = (0.5 - jnp.abs(reduced)) - 1.4e-8
    s2 = s * s
    p = jnp.float32(-0.00737043)
    for c in (0.082145887, -0.59926453, 2.5501640, -5.1677128, 3.1415927):
        p = p * s2 + jnp.float32(c)
    return p * s


def split(value):
    high = value.astype(BF16)
    return high, (value - high.astype(F32)).astype(BF16)


def kernel(
    meta,
    coords,
    weights,
    slave_hbm,
    master_hbm,
    out_master,
    out_slave,
    window,
    slave,
    mortar,
    dual,
    tables,
    first_sq,
    second_sq,
    run,
    mult,
    send_p,
    recv_p,
    send_o,
    recv_o,
    send_h,
    recv_h,
    stage,
    local_sem,
    out_sem,
    halo_h_send,
    halo_h_recv,
    halo_l_send,
    halo_l_recv,
    halo_f_send,
    halo_f_recv,
    force_l_send,
    force_l_recv,
    force_m_send,
    force_m_recv,
    force_h_send,
    force_h_recv,
):
    at_len = lax.axis_index("len")
    at_hgt = lax.axis_index("hgt")
    n_len = lax.axis_size("len")
    n_hgt = lax.axis_size("hgt")
    odd = lax.rem(at_len, 2)
    partner = (at_len + 1 - 2 * odd, at_hgt)
    other = (lax.rem(at_len - 1 + 2 * odd + n_len, n_len), at_hgt)
    above = (at_len, lax.rem(at_hgt + 1, n_hgt))
    below = (at_len, lax.rem(at_hgt + n_hgt - 1, n_hgt))

    def remote(src, dst, send_sem, recv_sem, device):
        return pltpu.make_async_remote_copy(
            src_ref=src,
            dst_ref=dst,
            send_sem=send_sem,
            recv_sem=recv_sem,
            device_id=device,
            device_id_type=MESH,
        )

    def faces(g):
        return pl.ds(g * PART, PART)

    def halo_up(g):
        return remote(
            master_hbm.at[faces(g)],
            window.at[OWN, DOWN, faces(g)],
            halo_h_send.at[0, g],
            halo_h_recv.at[0, g],
            above,
        )

    def halo_down(g):
        return remote(
            master_hbm.at[faces(g)],
            window.at[OWN, UP, faces(g)],
            halo_h_send.at[1, g],
            halo_h_recv.at[1, g],
            below,
        )

    def halo_own(column):
        return remote(
            master_hbm,
            window.at[column, MID],
            halo_l_send.at[column - 1],
            halo_l_recv.at[column - 1],
            partner if column == PARTNER else other,
        )

    def halo_forward(column, row, g):
        return remote(
            window.at[OWN, row, faces(g)],
            window.at[column, row, faces(g)],
            halo_f_send.at[column - 1, row, g],
            halo_f_recv.at[column - 1, row, g],
            partner if column == PARTNER else other,
        )

    def force_len(column, g):
        if column == PARTNER:
            src, dst, device = send_p, recv_p, partner
        else:
            src, dst, device = send_o, recv_o, other
        return remote(
            src.at[g, pl.ds(0, 2)],
            dst.at[g, pl.ds(0, 2)],
            force_l_send.at[column - 1, g],
            force_l_recv.at[column - 1, g],
            device,
        )

    def force_mid(column, g):
        if column == PARTNER:
            src, dst, device = send_p, recv_p, partner
        else:
            src, dst, device = send_o, recv_o, other
        return remote(
            src.at[g, MID],
            dst.at[g, MID],
            force_m_send.at[column - 1, g],
            force_m_recv.at[column - 1, g],
            device,
        )

    def force_hgt(row, g):
        return remote(
            send_h.at[row, g],
            recv_h.at[1 - row, g],
            force_h_send.at[row, g],
            force_h_recv.at[1 - row, g],
            below if row == DOWN else above,
        )

    barrier = pltpu.get_barrier_semaphore()
    for device in (partner, other, above, below):
        pl.semaphore_signal(barrier, inc=1, device_id=device, device_id_type=MESH)
    pl.semaphore_wait(barrier, 4)

    for column in (OTHER, PARTNER):
        halo_own(column).start()
    for g in range(CHUNKS):
        halo_up(g).start()
        halo_down(g).start()
    own_copy = pltpu.make_async_copy(master_hbm, window.at[OWN, MID], local_sem.at[0])
    own_copy.start()
    slave_copy = pltpu.make_async_copy(slave_hbm, slave, local_sem.at[1])
    slave_copy.start()

    modes = lax.broadcasted_iota(jnp.int32, (ORDER, NODES), 0).astype(F32)
    row_ids = lax.broadcasted_iota(jnp.int32, (NODES, NODES), 0)
    col_ids = lax.broadcasted_iota(jnp.int32, (NODES, NODES), 1)

    def build_tables(first_pair):
        def one(i, _):
            points = coords[first_pair + i]
            weight = weights[pl.ds(first_pair + i, 1), :]
            sx, sy, mx, my = (cos_pi(modes * points[k : k + 1]) for k in range(4))
            rows = pl.ds(pl.multiple_of(i * ORDER, ORDER), ORDER)
            tables[i, 0] = sx
            tables[i, 1] = sy
            tables[i, 2] = mx * weight
            tables[i, 3] = my
            first_sq[rows, :] = sx * sx * weight
            second_sq[rows, :] = sy * sy
            return 0

        lax.fori_loop(0, GROUP, one, 0)
        sums = lax.dot_general(
            first_sq[...],
            second_sq[...],
            NT,
            precision=lax.Precision.HIGHEST,
            preferred_element_type=F32,
        )
        sums = jnp.where(row_ids // ORDER == col_ids // ORDER, sums, 0.0)
        spread = jnp.where(row_ids % ORDER == col_ids % ORDER, 1.0, 0.0).astype(F32)
        wide = lax.dot_general(
            sums, spread, NN, precision=lax.Precision.HIGHEST, preferred_element_type=F32
        )
        wide = jnp.where(row_ids % ORDER == col_ids // ORDER, wide, 0.0)
        at = pl.ds(pl.multiple_of(first_pair, GROUP), GROUP)
        dual[at, :] = jnp.sum(wide.reshape(GROUP, ORDER, NODES), axis=1)

    def table_of(i, k):
        first, second = tables[i, k], tables[i, k + 1]
        return (first[:, None, :] * second[None, :, :]).reshape(NODES, NODES)

    def build_mortar(first_pair):
        def some(step, _):
            for u in range(LOCK_A):
                i = step * LOCK_A + u
                slave_high, slave_low = split(table_of(i, 0))
                master_high, master_low = split(table_of(i, 2))
                left = jnp.concatenate([slave_high, slave_low, slave_high], axis=1)
                right = jnp.concatenate([master_high, master_high, master_low], axis=1)
                product = lax.dot_general(left, right, NT, preferred_element_type=F32)
                mortar[first_pair + i] = product.astype(BF16)
            return 0

        lax.fori_loop(0, GROUP // LOCK_A, some, 0)

    def prepare(g, _):
        build_tables(g * GROUP)
        build_mortar(g * GROUP)
        halo_up(g).wait_recv()
        halo_down(g).wait_recv()
        for row in (DOWN, UP):
            for column in (OTHER, PARTNER):
                halo_forward(column, row, g).start()
        return 0

    lax.fori_loop(0, CHUNKS, prepare, 0)

    own_copy.wait()
    slave_copy.wait()
    for column in (PARTNER, OTHER):
        halo_own(column).wait_recv()

    def arrived(g, _):
        for row in (DOWN, UP):
            for column in (PARTNER, OTHER):
                halo_forward(column, row, g).wait_recv()
        return 0

    lax.fori_loop(0, CHUNKS, arrived, 0)

    def contact(step, _):
        slots = [step * LOCK_B + u for u in range(LOCK_B)]
        pairs = [meta[AT_PAIR + t] for t in slots]
        mortars = [mortar[p] for p in pairs]
        projected = []
        for t, matrix in zip(slots, mortars):
            spot = meta[AT_MASTER + t]
            block = spot // FACES
            master = window[block // 3, block % 3, spot % FACES]
            projected.append(lax.dot_general(master, matrix, NT, preferred_element_type=F32))
        multipliers = []
        for t, p, part in zip(slots, pairs, projected):
            diag = dual[pl.ds(p, 1), :]
            gap = slave[meta[AT_SLAVE + t]].astype(F32) * diag - part
            multipliers.append(jnp.where(meta[AT_LIVE + t] > 0, gap * (1.0 / diag), 0.0))
        pushes = [
            jnp.dot(m.astype(BF16), matrix, preferred_element_type=F32)
            for m, matrix in zip(multipliers, mortars)
        ]
        for t, m in zip(slots, multipliers):
            mult[t] = m
        total = run[jnp.maximum(slots[0] - 1, 0)]
        for t, push in zip(slots, pushes):
            total = jnp.where(meta[AT_KEEP + t] > 0, total, 0.0) + push
            run[t] = total
        return 0

    run[0] = jnp.zeros((CHANNELS, NODES), F32)
    lax.fori_loop(0, PAIRS // LOCK_B, contact, 0)

    def force(column, row, face):
        spot = (column * 3 + row) * FACES + face
        return jnp.where(meta[AT_HAS + spot] > 0, run[meta[AT_LAST + spot]], 0.0)

    def fill(g, rows):
        def one(i, _):
            for row in rows:
                send_p[g, row, i] = force(PARTNER, row, g * PART + i)
                send_o[g, row, i] = force(OTHER, row, g * PART + i).astype(BF16)
            return 0

        lax.fori_loop(0, PART, one, 0)

    def send_sides(g, _):
        fill(g, (DOWN, UP))
        for column in (OTHER, PARTNER):
            force_len(column, g).start()
        return 0

    def send_middle(g, _):
        fill(g, (MID,))
        for column in (OTHER, PARTNER):
            force_mid(column, g).start()
        return 0

    lax.fori_loop(0, CHUNKS, send_sides, 0)
    lax.fori_loop(0, CHUNKS, send_middle, 0)

    def add_slaves(face, _):
        def some(step, total):
            for u in range(LOCK_B):
                t = step * LOCK_B + u
                total = total + jnp.where(meta[AT_SLAVE + t] == face, mult[t], 0.0)
            return total

        start = jnp.zeros((CHANNELS, NODES), F32)
        out_slave[face] = lax.fori_loop(0, PAIRS // LOCK_B, some, start)
        return 0

    def send_heights(g, _):
        lax.fori_loop(g * PART, (g + 1) * PART, add_slaves, 0)
        for column in (PARTNER, OTHER):
            force_len(column, g).wait_recv()

        for i in range(PART):
            for row in (DOWN, UP):
                total = force(OWN, row, g * PART + i)
                total = total + recv_p[g, row, i] + recv_o[g, row, i].astype(F32)
                high = total.astype(BF16)
                send_h[row, g, i] = high
                if i < EXTRA:
                    send_h[row, g, PART + i] = (total - high.astype(F32)).astype(BF16)
        for row in (DOWN, UP):
            force_hgt(row, g).start()
        return 0

    lax.fori_loop(0, CHUNKS, send_heights, 0)

    def out_copy(g):
        return pltpu.make_async_copy(stage.at[faces(g)], out_master.at[faces(g)], out_sem.at[g])

    def finish(g, _):
        for column in (PARTNER, OTHER):
            force_mid(column, g).wait_recv()
        for row in (DOWN, UP):
            force_hgt(row, g).wait_recv()
        for i in range(PART):
            total = force(OWN, MID, g * PART + i)
            total = total + recv_p[g, MID, i] + recv_o[g, MID, i].astype(F32)
            for row in (DOWN, UP):
                total = total + recv_h[row, g, i].astype(F32)
                if i < EXTRA:
                    total = total + recv_h[row, g, PART + i].astype(F32)
            stage[g * PART + i] = total
        out_copy(g).start()
        return 0

    lax.fori_loop(0, CHUNKS, finish, 0)

    for column in (PARTNER, OTHER):
        halo_own(column).wait_send()

    def sent(g, _):
        halo_up(g).wait_send()
        halo_down(g).wait_send()
        for column in (PARTNER, OTHER):
            for row in (DOWN, UP):
                halo_forward(column, row, g).wait_send()
            force_len(column, g).wait_send()
            force_mid(column, g).wait_send()
        for row in (DOWN, UP):
            force_hgt(row, g).wait_send()
        out_copy(g).wait()
        return 0

    lax.fori_loop(0, CHUNKS, sent, 0)


def order_pairs(pair_count, slave_face, master_row, master_col, active):
    side = 4
    band_len, band_hgt = lax.axis_index("len"), lax.axis_index("hgt")
    slots = jnp.arange(PAIRS, dtype=jnp.int32)
    live = (slots < pair_count) & (active == 1)
    step_len = master_row // side - band_len
    step_hgt = master_col // side - band_hgt
    column = jnp.where(step_len == 0, OWN, jnp.where(step_len == 1 - 2 * (band_len % 2), PARTNER, OTHER))
    row = jnp.where(step_hgt == 0, MID, jnp.where(step_hgt < 0, DOWN, UP))
    spot = (column * 3 + row) * FACES + (master_row % side) * side + master_col % side
    key = jnp.where(live, spot, SPOTS)
    before = (key[None, :] < key[:, None]) | ((key[None, :] == key[:, None]) & (slots[None, :] < slots[:, None]))
    rank = jnp.sum(before.astype(jnp.int32), axis=1)
    chosen = rank[None, :] == slots[:, None]

    def pick(values):
        return jnp.sum(jnp.where(chosen, values[None, :], 0), axis=1)

    sorted_key = pick(key)
    keep = jnp.concatenate([jnp.zeros((1,), bool), sorted_key[1:] == sorted_key[:-1]])
    spots = jnp.arange(SPOTS, dtype=jnp.int32)
    has = jnp.sum((key[None, :] == spots[:, None]).astype(jnp.int32), axis=1)
    last = jnp.sum((key[None, :] <= spots[:, None]).astype(jnp.int32), axis=1) - 1
    return jnp.concatenate(
        [
            pick(slots),
            jnp.where(sorted_key < SPOTS, sorted_key, 0),
            pick(slave_face),
            (sorted_key < SPOTS).astype(jnp.int32),
            keep.astype(jnp.int32),
            jnp.maximum(last, 0),
            has,
        ]
    )


def body(
    slave_disp,
    master_disp,
    quad_coords,
    quad_weights,
    pair_count,
    slave_face,
    master_row,
    master_col,
    active,
):
    meta = order_pairs(
        pair_count[0, 0], slave_face[0, 0], master_row[0, 0], master_col[0, 0], active[0, 0]
    )
    face = (CHANNELS, NODES)
    dma = pltpu.SemaphoreType.DMA
    out = jax.ShapeDtypeStruct((FACES, *face), F32)
    vmem = pl.BlockSpec(memory_space=pltpu.VMEM)
    hbm = pl.BlockSpec(memory_space=pl.ANY)
    master_force, slave_sum = pl.pallas_call(
        kernel,
        out_shape=(out, out),
        in_specs=[pl.BlockSpec(memory_space=pltpu.SMEM), vmem, vmem, hbm, hbm],
        out_specs=(hbm, vmem),
        scratch_shapes=[
            pltpu.VMEM((3, 3, FACES, *face), BF16),
            pltpu.VMEM((FACES, *face), BF16),
            pltpu.VMEM((PAIRS, NODES, NODES), BF16),
            pltpu.VMEM((PAIRS, NODES), F32),
            pltpu.VMEM((GROUP, 4, ORDER, NODES), F32),
            pltpu.VMEM((NODES, NODES), F32),
            pltpu.VMEM((NODES, NODES), F32),
            pltpu.VMEM((PAIRS, *face), F32),
            pltpu.VMEM((PAIRS, *face), F32),
            pltpu.VMEM((CHUNKS, 3, PART, *face), F32),
            pltpu.VMEM((CHUNKS, 3, PART, *face), F32),
            pltpu.VMEM((CHUNKS, 3, PART, *face), BF16),
            pltpu.VMEM((CHUNKS, 3, PART, *face), BF16),
            pltpu.VMEM((2, CHUNKS, PART + EXTRA, *face), BF16),
            pltpu.VMEM((2, CHUNKS, PART + EXTRA, *face), BF16),
            pltpu.VMEM((FACES, *face), F32),
            dma((2,)),
            dma((CHUNKS,)),
            dma((2, CHUNKS)),
            dma((2, CHUNKS)),
            dma((2,)),
            dma((2,)),
            dma((2, 2, CHUNKS)),
            dma((2, 2, CHUNKS)),
            dma((2, CHUNKS)),
            dma((2, CHUNKS)),
            dma((2, CHUNKS)),
            dma((2, CHUNKS)),
            dma((2, CHUNKS)),
            dma((2, CHUNKS)),
        ],
        compiler_params=pltpu.CompilerParams(
            collective_id=0, has_side_effects=True, vmem_limit_bytes=60 * 2**20
        ),
    )(
        meta,
        quad_coords.reshape(PAIRS, 4, NODES),
        quad_weights.reshape(PAIRS, NODES),
        slave_disp.reshape(FACES, *face),
        master_disp.reshape(FACES, *face),
    )
    return (
        master_force.reshape(4, 4, *face),
        slave_sum.reshape(4, 4, *face),
    )


def solution(mesh):
    in_specs = (
        P("len", "hgt", None, None),
        P("len", "hgt", None, None),
        P("len", "hgt", None, None, None),
        P("len", "hgt", None, None),
        P("len", "hgt"),
        P("len", "hgt", None),
        P("len", "hgt", None),
        P("len", "hgt", None),
        P("len", "hgt", None),
    )
    out_specs = (P("len", "hgt", None, None), P("len", "hgt", None, None))
    return jax.shard_map(body, mesh=mesh, in_specs=in_specs, out_specs=out_specs, check_vma=False)
```

```python
import functools

import jax
import jax.numpy as jnp
from jax import lax
from jax.experimental import pallas as pl
from jax.experimental.pallas import tpu as pltpu
from jax.sharding import PartitionSpec as P

ORDER = 16
NODES = 256
CHANNELS = 96
FACES = 16
PAIRS = 64
GROUP = 16
LOCK_A = 4
LOCK_B = 8
CHUNKS = 4
PART = FACES // CHUNKS
F32, BF16 = jnp.float32, jnp.bfloat16
MESH = pl.DeviceIdType.MESH
NT = (((1,), (1,)), ((), ()))
NN = (((1,), (0,)), ((), ()))

OWN, PARTNER, OTHER = range(3)
DOWN, UP, MID = range(3)
BLOCKS = 9
SPOTS = BLOCKS * FACES

AT_PAIR, AT_MASTER, AT_SLAVE, AT_LAST = range(4)
META = (8, 256)
TURN = CHUNKS - 1


def cos_pi(turns):
    reduced = turns - 2.0 * jnp.round(turns * 0.5)
    s = (0.5 - jnp.abs(reduced)) - 1.4e-8
    s2 = s * s
    p = jnp.float32(-0.00737043)
    for c in (0.082145887, -0.59926453, 2.5501640, -5.1677128, 3.1415927):
        p = p * s2 + jnp.float32(c)
    return p * s


def split(value):
    high = value.astype(BF16)
    return high, (value - high.astype(F32)).astype(BF16)


def order_pairs(pair_count, ints, order):
    side = 4
    at_len, at_hgt = lax.axis_index("len"), lax.axis_index("hgt")
    square = (PAIRS, PAIRS)
    down, along = (lax.broadcasted_iota(jnp.int32, square, d) for d in (0, 1))
    slots = lax.broadcasted_iota(jnp.int32, (1, PAIRS), 1)
    slave_face, master_row, master_col, active = (ref[...] for ref in ints)
    live = (slots < pair_count[0, 0]) & (active == 1)
    step_len = master_row // side - at_len
    step_hgt = master_col // side - at_hgt
    column = jnp.where(step_len == 0, OWN, jnp.where(step_len == 1 - 2 * lax.rem(at_len, 2), PARTNER, OTHER))
    row = jnp.where(step_hgt == 0, MID, jnp.where(step_hgt < 0, DOWN, UP))
    spot = (column * 3 + row) * FACES + (master_row % side) * side + master_col % side
    key = jnp.where(live, spot, SPOTS)

    def stand(values):
        return jnp.sum(jnp.where(down == along, values, 0), axis=1, keepdims=True)

    key_col = stand(key)
    before = (key < key_col) | ((key == key_col) & (along < down))
    rank = jnp.sum(before.astype(jnp.int32), axis=1, keepdims=True)
    chosen = rank == along

    def pick(values):
        return jnp.sum(jnp.where(chosen, values, 0), axis=0, keepdims=True)

    spots = lax.broadcasted_iota(jnp.int32, (PAIRS, META[1]), 1)
    has = jnp.sum((key_col == spots).astype(jnp.int32), axis=0, keepdims=True)
    upto = jnp.sum((key_col <= spots).astype(jnp.int32), axis=0, keepdims=True)
    order[...] = jnp.zeros(META, jnp.int32)
    order[AT_PAIR : AT_PAIR + 1, :PAIRS] = pick(down)
    order[AT_MASTER : AT_MASTER + 1, :PAIRS] = pick(key_col)
    order[AT_SLAVE : AT_SLAVE + 1, :PAIRS] = pick(stand(slave_face))
    order[AT_LAST : AT_LAST + 1, :] = jnp.where(has > 0, upto - 1, -1)


def kernel(
    pair_count,
    slave_face,
    master_row,
    master_col,
    active,
    coords,
    weights,
    slave_hbm,
    master_hbm,
    out_master,
    out_slave,
    order,
    meta,
    points,
    point_weights,
    window,
    slave,
    mortar,
    dual,
    tables,
    first_sq,
    second_sq,
    run,
    mult,
    send_p,
    recv_p,
    send_o,
    recv_o,
    recv_d,
    send_h,
    recv_h,
    local_sem,
    halo_h_send,
    halo_h_recv,
    halo_p_send,
    halo_p_recv,
    halo_o_send,
    halo_o_recv,
    halo_d_send,
    halo_d_recv,
    halo_f_send,
    halo_f_recv,
    force_l_send,
    force_l_recv,
    force_m_send,
    force_m_recv,
    force_d_send,
    force_d_recv,
    force_h_send,
    force_h_recv,
):
    at_len = lax.axis_index("len")
    at_hgt = lax.axis_index("hgt")
    n_len = lax.axis_size("len")
    n_hgt = lax.axis_size("hgt")
    odd = lax.rem(at_len, 2)
    other_len = at_len - 1 + 2 * odd
    partner = (at_len + 1 - 2 * odd, at_hgt)
    other = (lax.rem(other_len + n_len, n_len), at_hgt)
    above = (at_len, lax.rem(at_hgt + 1, n_hgt))
    below = (at_len, lax.rem(at_hgt + n_hgt - 1, n_hgt))
    has_other = (other_len >= 0) & (other_len < n_len)
    has_row = (at_hgt > 0, at_hgt < n_hgt - 1)
    beside = (below, above)
    neighbours = ((partner, None), (other, has_other), (below, has_row[DOWN]), (above, has_row[UP]))

    def when(condition, action):
        if condition is None:
            action()
        else:
            pl.when(condition)(action)

    def both(first, second):
        return second if first is None else first & second

    def remote(src, dst, send_sem, recv_sem, device):
        return pltpu.make_async_remote_copy(
            src_ref=src,
            dst_ref=dst,
            send_sem=send_sem,
            recv_sem=recv_sem,
            device_id=device,
            device_id_type=MESH,
        )

    def faces(g):
        return pl.ds(g * PART, PART)

    def halo_hgt(row, g):
        return remote(
            master_hbm.at[faces(g)],
            window.at[OWN, 1 - row, faces(g)],
            halo_h_send.at[row, g],
            halo_h_recv.at[1 - row, g],
            beside[row],
        )

    def halo_partner():
        return remote(
            master_hbm, window.at[PARTNER, MID], halo_p_send.at[0], halo_p_recv.at[0], partner
        )

    def halo_other(g):
        return remote(
            master_hbm.at[faces(g)],
            window.at[OTHER, MID, faces(g)],
            halo_o_send.at[g],
            halo_o_recv.at[g],
            other,
        )

    def halo_turn(row):
        return remote(
            window.at[OTHER, MID, faces(TURN)],
            window.at[OTHER, 1 - row, faces(TURN)],
            halo_d_send.at[row],
            halo_d_recv.at[1 - row],
            beside[row],
        )

    def halo_forward(column, row, g):
        return remote(
            window.at[OWN, row, faces(g)],
            window.at[column, row, faces(g)],
            halo_f_send.at[column - 1, row, g],
            halo_f_recv.at[column - 1, row, g],
            partner if column == PARTNER else other,
        )

    def force_len(column, g):
        if column == PARTNER:
            src, dst, device = send_p, recv_p, partner
        else:
            src, dst, device = send_o, recv_o, other
        return remote(
            src.at[g, pl.ds(0, 2)],
            dst.at[g, pl.ds(0, 2)],
            force_l_send.at[column - 1, g],
            force_l_recv.at[column - 1, g],
            device,
        )

    def force_mid(column, g):
        if column == PARTNER:
            src, dst, device = send_p, recv_p, partner
        else:
            src, dst, device = send_o, recv_o, other
        return remote(
            src.at[g, MID],
            dst.at[g, MID],
            force_m_send.at[column - 1, g],
            force_m_recv.at[column - 1, g],
            device,
        )

    def force_turn(row):
        return remote(
            send_o.at[TURN, row],
            recv_d.at[1 - row],
            force_d_send.at[row],
            force_d_recv.at[1 - row],
            beside[row],
        )

    def force_hgt(row, g):
        return remote(
            send_h.at[row, g],
            recv_h.at[1 - row, g],
            force_h_send.at[row, g],
            force_h_recv.at[1 - row, g],
            beside[row],
        )

    barrier = pltpu.get_barrier_semaphore()
    for device, there in neighbours:

        def greet(device=device):
            pl.semaphore_signal(barrier, inc=1, device_id=device, device_id_type=MESH)

        when(there, greet)
    loads = [
        pltpu.make_async_copy(coords, points, local_sem.at[0]),
        pltpu.make_async_copy(weights, point_weights, local_sem.at[1]),
        pltpu.make_async_copy(master_hbm, window.at[OWN, MID], local_sem.at[2]),
        pltpu.make_async_copy(slave_hbm, slave, local_sem.at[3]),
    ]
    for load in loads:
        load.start()
    pl.semaphore_wait(barrier, 1 + sum(there.astype(jnp.int32) for _, there in neighbours[1:]))

    @pl.when(has_other)
    def _():
        for g in (TURN, *range(TURN)):
            halo_other(g).start()

    halo_partner().start()
    for g in range(CHUNKS):
        for row in (DOWN, UP):
            when(has_row[row], lambda row=row, g=g: halo_hgt(row, g).start())

    order_pairs(pair_count, (slave_face, master_row, master_col, active), order)
    publish = pltpu.make_async_copy(order, meta, local_sem.at[4])
    publish.start()
    loads[0].wait()
    loads[1].wait()

    modes = lax.broadcasted_iota(jnp.int32, (ORDER, NODES), 0).astype(F32)
    row_ids = lax.broadcasted_iota(jnp.int32, (NODES, NODES), 0)
    col_ids = lax.broadcasted_iota(jnp.int32, (NODES, NODES), 1)

    def build_tables(first_pair):
        def one(i, _):
            place = points[first_pair + i]
            weight = point_weights[pl.ds(first_pair + i, 1), :]
            sx, sy, mx, my = (cos_pi(modes * place[k : k + 1]) for k in range(4))
            rows = pl.ds(pl.multiple_of(i * ORDER, ORDER), ORDER)
            tables[i, 0] = sx
            tables[i, 1] = sy
            tables[i, 2] = mx * weight
            tables[i, 3] = my
            first_sq[rows, :] = sx * sx * weight
            second_sq[rows, :] = sy * sy
            return 0

        lax.fori_loop(0, GROUP, one, 0)
        sums = lax.dot_general(
            first_sq[...],
            second_sq[...],
            NT,
            precision=lax.Precision.HIGHEST,
            preferred_element_type=F32,
        )
        sums = jnp.where(row_ids // ORDER == col_ids // ORDER, sums, 0.0)
        spread = jnp.where(row_ids % ORDER == col_ids % ORDER, 1.0, 0.0).astype(F32)
        wide = lax.dot_general(
            sums, spread, NN, precision=lax.Precision.HIGHEST, preferred_element_type=F32
        )
        wide = jnp.where(row_ids % ORDER == col_ids // ORDER, wide, 0.0)
        at = pl.ds(pl.multiple_of(first_pair, GROUP), GROUP)
        dual[at, :] = jnp.sum(wide.reshape(GROUP, ORDER, NODES), axis=1)

    def table_of(i, k):
        first, second = tables[i, k], tables[i, k + 1]
        return (first[:, None, :] * second[None, :, :]).reshape(NODES, NODES)

    def build_mortar(first_pair):
        def some(step, _):
            for u in range(LOCK_A):
                i = step * LOCK_A + u
                slave_high, slave_low = split(table_of(i, 0))
                master_high, master_low = split(table_of(i, 2))
                left = jnp.concatenate([slave_high, slave_low, slave_high], axis=1)
                right = jnp.concatenate([master_high, master_high, master_low], axis=1)
                product = lax.dot_general(left, right, NT, preferred_element_type=F32)
                mortar[first_pair + i] = product.astype(BF16)
            return 0

        lax.fori_loop(0, GROUP // LOCK_A, some, 0)

    def prepare(g, _):
        build_tables(g * GROUP)
        build_mortar(g * GROUP)

        @pl.when((g == 0) & has_other)
        def _():
            halo_other(TURN).wait_recv()
            for row in (DOWN, UP):
                when(has_row[row], lambda row=row: halo_turn(row).start())

        for row in (DOWN, UP):

            def pass_on(row=row):
                halo_hgt(1 - row, g).wait_recv()
                pl.when(has_other & (g != TURN))(lambda: halo_forward(OTHER, row, g).start())
                halo_forward(PARTNER, row, g).start()

            when(has_row[row], pass_on)
        return 0

    lax.fori_loop(0, CHUNKS, prepare, 0)

    publish.wait()
    loads[2].wait()
    loads[3].wait()
    halo_partner().wait_recv()

    def arrived(g, _):
        pl.when(has_other)(lambda: halo_other_rest(g))
        for row in (DOWN, UP):

            def rest(row=row):
                halo_forward(PARTNER, row, g).wait_recv()
                pl.when(has_other & (g != TURN))(lambda: halo_forward(OTHER, row, g).wait_recv())
                pl.when(has_other & (g == TURN))(lambda: halo_turn(1 - row).wait_recv())

            when(has_row[row], rest)
        return 0

    def halo_other_rest(g):
        pl.when(g != TURN)(lambda: halo_other(g).wait_recv())

    lax.fori_loop(0, CHUNKS, arrived, 0)

    @pl.when(jnp.logical_not(has_other))
    def _():
        recv_o[...] = jnp.zeros(recv_o.shape, BF16)

    for row in (DOWN, UP):

        @pl.when(jnp.logical_not(has_row[row]))
        def _(row=row):
            recv_h[row] = jnp.zeros(recv_h.shape[1:], BF16)
            recv_d[row] = jnp.zeros(recv_d.shape[1:], BF16)

    def contact(step, _):
        slots = [step * LOCK_B + u for u in range(LOCK_B)]
        pairs = [meta[AT_PAIR, t] for t in slots]
        keys = [meta[AT_MASTER, t] for t in slots]
        mortars = [mortar[p] for p in pairs]
        projected = []
        for key, matrix in zip(keys, mortars):
            spot = jnp.where(key < SPOTS, key, MID * FACES)
            block = spot // FACES
            master = window[block // 3, block % 3, spot % FACES]
            projected.append(lax.dot_general(master, matrix, NT, preferred_element_type=F32))
        multipliers = []
        for t, p, key, part in zip(slots, pairs, keys, projected):
            diag = dual[pl.ds(p, 1), :]
            gap = slave[meta[AT_SLAVE, t]].astype(F32) * diag - part
            multipliers.append(jnp.where(key < SPOTS, gap * (1.0 / diag), 0.0))
        pushes = [
            jnp.dot(m.astype(BF16), matrix, preferred_element_type=F32)
            for m, matrix in zip(multipliers, mortars)
        ]
        for t, m in zip(slots, multipliers):
            mult[t] = m
        total = run[jnp.maximum(slots[0] - 1, 0)]
        last = meta[AT_MASTER, jnp.maximum(slots[0] - 1, 0)]
        for t, key, push in zip(slots, keys, pushes):
            total = jnp.where(key == last, total, 0.0) + push
            run[t] = total
            last = key
        return 0

    run[0] = jnp.zeros((CHANNELS, NODES), F32)
    lax.fori_loop(0, PAIRS // LOCK_B, contact, 0)

    def force(column, row, face):
        last = meta[AT_LAST, (column * 3 + row) * FACES + face]
        return jnp.where(last >= 0, run[jnp.maximum(last, 0)], 0.0)

    def fill(column, g, rows):
        send = send_p if column == PARTNER else send_o

        def one(i, _):
            for row in rows:
                send[g, row, i] = force(column, row, g * PART + i).astype(send.dtype)
            return 0

        lax.fori_loop(0, PART, one, 0)

    def to_other(action):
        pl.when(has_other)(action)

    fill(OTHER, TURN, (DOWN, UP))
    for row in (DOWN, UP):
        when(has_row[row], lambda row=row: force_turn(row).start())

    def send_sides(g, _):
        fill(OTHER, g, (DOWN, UP))
        to_other(lambda: force_len(OTHER, g).start())
        return 0

    def send_partner(k, _):
        g = lax.rem(k + TURN, CHUNKS)
        fill(PARTNER, g, (DOWN, UP))
        force_len(PARTNER, g).start()
        return 0

    def send_middle(g, _):
        fill(OTHER, g, (MID,))
        to_other(lambda: force_mid(OTHER, g).start())
        return 0

    def send_partner_middle(g, _):
        fill(PARTNER, g, (MID,))
        force_mid(PARTNER, g).start()
        return 0

    lax.fori_loop(0, 1, send_sides, 0)
    lax.fori_loop(0, 1, send_partner, 0)
    lax.fori_loop(1, TURN, send_sides, 0)
    lax.fori_loop(1, CHUNKS, send_partner, 0)
    lax.fori_loop(0, TURN, send_middle, 0)
    lax.fori_loop(0, CHUNKS, send_partner_middle, 0)

    def add_slaves(face, _):
        def some(step, total):
            for u in range(LOCK_B):
                t = step * LOCK_B + u
                total = total + jnp.where(meta[AT_SLAVE, t] == face, mult[t], 0.0)
            return total

        start = jnp.zeros((CHANNELS, NODES), F32)
        out_slave[face] = lax.fori_loop(0, PAIRS // LOCK_B, some, start)
        return 0

    def send_heights(k, _):
        g = lax.rem(k + TURN, CHUNKS)
        force_len(PARTNER, g).wait_recv()
        for row in (DOWN, UP):
            for i in range(PART):
                total = force(OWN, row, g * PART + i) + recv_p[g, row, i]
                send_h[row, g, i] = total.astype(BF16)

        @pl.when(g != TURN)
        def _():
            to_other(lambda: force_len(OTHER, g).wait_recv())
            for row in (DOWN, UP):
                for i in range(PART):
                    total = force(OWN, row, g * PART + i) + recv_p[g, row, i]
                    send_h[row, g, i] = (total + recv_o[g, row, i].astype(F32)).astype(BF16)

        for row in (DOWN, UP):
            when(has_row[row], lambda row=row: force_hgt(row, g).start())

        @pl.when(g == TURN)
        def _():
            for row in (DOWN, UP):
                when(has_row[row], lambda row=row: force_turn(1 - row).wait_recv())
            for i in range(PART):
                total = force(OTHER, MID, g * PART + i)
                for row in (DOWN, UP):
                    total = total + recv_d[row, i].astype(F32)
                send_o[g, MID, i] = total.astype(BF16)
            to_other(lambda: force_mid(OTHER, g).start())

        lax.fori_loop(k * PART, (k + 1) * PART, add_slaves, 0)
        return 0

    lax.fori_loop(0, CHUNKS, send_heights, 0)

    def finish(g, _):
        force_mid(PARTNER, g).wait_recv()
        to_other(lambda: force_mid(OTHER, g).wait_recv())
        for row in (DOWN, UP):
            when(has_row[row], lambda row=row: force_hgt(1 - row, g).wait_recv())
        for i in range(PART):
            total = force(OWN, MID, g * PART + i)
            total = total + recv_p[g, MID, i] + recv_o[g, MID, i].astype(F32)
            for row in (DOWN, UP):
                total = total + recv_h[row, g, i].astype(F32)
            out_master[g * PART + i] = total
        return 0

    lax.fori_loop(0, CHUNKS, finish, 0)

    halo_partner().wait_send()
    for row in (DOWN, UP):
        when(has_row[row], lambda row=row: force_turn(row).wait_send())
        when(has_row[row] & has_other, lambda row=row: halo_turn(row).wait_send())

    def sent(g, _):
        to_other(lambda: halo_other(g).wait_send())
        force_len(PARTNER, g).wait_send()
        force_mid(PARTNER, g).wait_send()
        to_other(lambda: force_mid(OTHER, g).wait_send())
        pl.when(has_other & (g != TURN))(lambda: force_len(OTHER, g).wait_send())
        for row in (DOWN, UP):

            def rest(row=row):
                halo_hgt(row, g).wait_send()
                force_hgt(row, g).wait_send()
                halo_forward(PARTNER, row, g).wait_send()
                pl.when(has_other & (g != TURN))(lambda: halo_forward(OTHER, row, g).wait_send())

            when(has_row[row], rest)
        return 0

    lax.fori_loop(0, CHUNKS, sent, 0)


def store(master_in, slave_in, master_out, slave_out, sem):
    copies = [
        pltpu.make_async_copy(master_in, master_out, sem.at[0]),
        pltpu.make_async_copy(slave_in, slave_out, sem.at[1]),
    ]
    for copy in copies:
        copy.start()
    for copy in copies:
        copy.wait()


def body(
    slave_disp,
    master_disp,
    quad_coords,
    quad_weights,
    pair_count,
    slave_face,
    master_row,
    master_col,
    active,
):
    face = (CHANNELS, NODES)
    dma = pltpu.SemaphoreType.DMA
    out = jax.ShapeDtypeStruct((FACES, *face), F32)
    held = pltpu.VMEM((FACES, *face), F32)
    vmem = pl.BlockSpec(memory_space=pltpu.VMEM)
    hbm = pl.BlockSpec(memory_space=pl.ANY)
    slots = (1, PAIRS)
    results = pl.pallas_call(
        kernel,
        out_shape=(held, held),
        in_specs=[pl.BlockSpec(memory_space=pltpu.SMEM), *[vmem] * 4, *[hbm] * 4],
        out_specs=(vmem, vmem),
        scratch_shapes=[
            pltpu.VMEM(META, jnp.int32),
            pltpu.SMEM(META, jnp.int32),
            pltpu.VMEM((PAIRS, 4, NODES), F32),
            pltpu.VMEM((PAIRS, NODES), F32),
            pltpu.VMEM((3, 3, FACES, *face), BF16),
            pltpu.VMEM((FACES, *face), BF16),
            pltpu.VMEM((PAIRS, NODES, NODES), BF16),
            pltpu.VMEM((PAIRS, NODES), F32),
            pltpu.VMEM((GROUP, 4, ORDER, NODES), F32),
            pltpu.VMEM((NODES, NODES), F32),
            pltpu.VMEM((NODES, NODES), F32),
            pltpu.VMEM((PAIRS, *face), F32),
            pltpu.VMEM((PAIRS, *face), F32),
            pltpu.VMEM((CHUNKS, 3, PART, *face), F32),
            pltpu.VMEM((CHUNKS, 3, PART, *face), F32),
            pltpu.VMEM((CHUNKS, 3, PART, *face), BF16),
            pltpu.VMEM((CHUNKS, 3, PART, *face), BF16),
            pltpu.VMEM((2, PART, *face), BF16),
            pltpu.VMEM((2, CHUNKS, PART, *face), BF16),
            pltpu.VMEM((2, CHUNKS, PART, *face), BF16),
            dma((5,)),
            *[dma((2, CHUNKS))] * 2,
            *[dma((1,))] * 2,
            *[dma((CHUNKS,))] * 2,
            *[dma((2,))] * 2,
            *[dma((2, 2, CHUNKS))] * 2,
            *[dma((2, CHUNKS))] * 2,
            *[dma((2, CHUNKS))] * 2,
            *[dma((2,))] * 2,
            *[dma((2, CHUNKS))] * 2,
        ],
        compiler_params=pltpu.CompilerParams(
            collective_id=0, has_side_effects=True, vmem_limit_bytes=56 * 2**20
        ),
        name="contact",
    )(
        pair_count,
        slave_face.reshape(slots),
        master_row.reshape(slots),
        master_col.reshape(slots),
        active.reshape(slots),
        quad_coords.reshape(PAIRS, 4, NODES),
        quad_weights.reshape(PAIRS, NODES),
        slave_disp.reshape(FACES, *face),
        master_disp.reshape(FACES, *face),
    )
    results = [pltpu.with_memory_space_constraint(r, pltpu.VMEM) for r in results]
    master_force, slave_sum = pl.pallas_call(
        store,
        out_shape=(out, out),
        in_specs=[vmem, vmem],
        out_specs=(hbm, hbm),
        scratch_shapes=[dma((2,))],
        compiler_params=pltpu.CompilerParams(vmem_limit_bytes=2**20),
        name="store",
    )(*results)
    return (
        master_force.reshape(4, 4, *face),
        slave_sum.reshape(4, 4, *face),
    )


def solution(mesh):
    in_specs = (
        P("len", "hgt", None, None),
        P("len", "hgt", None, None),
        P("len", "hgt", None, None, None),
        P("len", "hgt", None, None),
        P("len", "hgt"),
        P("len", "hgt", None),
        P("len", "hgt", None),
        P("len", "hgt", None),
        P("len", "hgt", None),
    )
    out_specs = (P("len", "hgt", None, None), P("len", "hgt", None, None))
    return jax.shard_map(body, mesh=mesh, in_specs=in_specs, out_specs=out_specs, check_vma=False)
```

```python
import functools

import jax
import jax.numpy as jnp
from jax import lax
from jax.experimental import pallas as pl
from jax.experimental.pallas import tpu as pltpu
from jax.sharding import PartitionSpec as P

ORDER = 16
NODES = 256
CHANNELS = 96
FACES = 16
PAIRS = 64
GROUP = 16
LOCK_A = 8
LOCK_S = 8
LOCK_B = 16
CHUNKS = 4
HALVES = 2
ROWS = CHANNELS // HALVES
PART = FACES // CHUNKS
F32, BF16 = jnp.float32, jnp.bfloat16
MESH = pl.DeviceIdType.MESH
NT = (((1,), (1,)), ((), ()))
NN = (((1,), (0,)), ((), ()))

OWN, PARTNER, OTHER = range(3)
DOWN, UP, MID = range(3)
BLOCKS = 9
SPOTS = BLOCKS * FACES

AT_PAIR, AT_MASTER, AT_SLAVE, AT_LAST = range(4)
AT_TURN, AT_FACE, AT_END = range(4, 7)
META = (8, 256)
TURN = CHUNKS - 1


def cos_pi(turns):
    reduced = turns - 2.0 * jnp.round(turns * 0.5)
    s = (0.5 - jnp.abs(reduced)) - 1.4e-8
    s2 = s * s
    p = jnp.float32(-0.00737043)
    for c in (0.082145887, -0.59926453, 2.5501640, -5.1677128, 3.1415927):
        p = p * s2 + jnp.float32(c)
    return p * s


def split(value):
    high = value.astype(BF16)
    return high, (value - high.astype(F32)).astype(BF16)


def order_pairs(pair_count, ints, order):
    side = 4
    at_len, at_hgt = lax.axis_index("len"), lax.axis_index("hgt")
    square = (PAIRS, PAIRS)
    down, along = (lax.broadcasted_iota(jnp.int32, square, d) for d in (0, 1))
    slots = lax.broadcasted_iota(jnp.int32, (1, PAIRS), 1)
    slave_face, master_row, master_col, active = (ref[...] for ref in ints)
    live = (slots < pair_count[0, 0]) & (active == 1)
    step_len = master_row // side - at_len
    step_hgt = master_col // side - at_hgt
    column = jnp.where(step_len == 0, OWN, jnp.where(step_len == 1 - 2 * lax.rem(at_len, 2), PARTNER, OTHER))
    row = jnp.where(step_hgt == 0, MID, jnp.where(step_hgt < 0, DOWN, UP))
    spot = (column * 3 + row) * FACES + (master_row % side) * side + master_col % side
    key = jnp.where(live, spot, SPOTS)

    def stand(values):
        return jnp.sum(jnp.where(down == along, values, 0), axis=1, keepdims=True)

    def rank_of(key, key_col):
        before = (key < key_col) | ((key == key_col) & (along < down))
        return jnp.sum(before.astype(jnp.int32), axis=1, keepdims=True)

    def pick(rank, values):
        return jnp.sum(jnp.where(rank == along, values, 0), axis=0, keepdims=True)

    spots = lax.broadcasted_iota(jnp.int32, (PAIRS, META[1]), 1)

    def last_of(key_col):
        has = jnp.sum((key_col == spots).astype(jnp.int32), axis=0, keepdims=True)
        upto = jnp.sum((key_col <= spots).astype(jnp.int32), axis=0, keepdims=True)
        return jnp.where(has > 0, upto - 1, -1)

    key_col = stand(key)
    rank = rank_of(key, key_col)
    face_key = jnp.where(live, slave_face, FACES)
    face_col = stand(face_key)
    face_rank = rank_of(face_key, face_col)
    order[...] = jnp.zeros(META, jnp.int32)
    order[AT_PAIR : AT_PAIR + 1, :PAIRS] = pick(rank, down)
    order[AT_MASTER : AT_MASTER + 1, :PAIRS] = pick(rank, key_col)
    order[AT_SLAVE : AT_SLAVE + 1, :PAIRS] = pick(rank, stand(slave_face))
    order[AT_LAST : AT_LAST + 1, :] = last_of(key_col)
    order[AT_TURN : AT_TURN + 1, :PAIRS] = pick(face_rank, rank)
    order[AT_FACE : AT_FACE + 1, :PAIRS] = pick(face_rank, face_col)
    order[AT_END : AT_END + 1, :] = last_of(face_col)


def kernel(
    pair_count,
    slave_face,
    master_row,
    master_col,
    active,
    coords,
    weights,
    slave_hbm,
    master_hbm,
    out_master,
    out_slave,
    order,
    meta,
    points,
    point_weights,
    window_first,
    window_second,
    slave,
    mortar,
    dual,
    tables,
    first_sq,
    second_sq,
    run,
    mult,
    slave_run,
    send_p,
    recv_p,
    send_o,
    recv_o,
    recv_d,
    send_h,
    recv_h,
    local_sem,
    halo_h_send,
    halo_h_recv,
    halo_p_send,
    halo_p_recv,
    halo_o_send,
    halo_o_recv,
    halo_d_send,
    halo_d_recv,
    halo_f_send,
    halo_f_recv,
    force_l_send,
    force_l_recv,
    force_m_send,
    force_m_recv,
    force_d_send,
    force_d_recv,
    force_h_send,
    force_h_recv,
):
    windows = (window_first, window_second)
    at_len = lax.axis_index("len")
    at_hgt = lax.axis_index("hgt")
    n_len = lax.axis_size("len")
    n_hgt = lax.axis_size("hgt")
    odd = lax.rem(at_len, 2)
    other_len = at_len - 1 + 2 * odd
    partner = (at_len + 1 - 2 * odd, at_hgt)
    other = (lax.rem(other_len + n_len, n_len), at_hgt)
    above = (at_len, lax.rem(at_hgt + 1, n_hgt))
    below = (at_len, lax.rem(at_hgt + n_hgt - 1, n_hgt))
    has_other = (other_len >= 0) & (other_len < n_len)
    has_row = (at_hgt > 0, at_hgt < n_hgt - 1)
    beside = (below, above)
    neighbours = ((partner, None), (other, has_other), (below, has_row[DOWN]), (above, has_row[UP]))

    def when(condition, action):
        if condition is None:
            action()
        else:
            pl.when(condition)(action)

    def remote(src, dst, send_sem, recv_sem, device):
        return pltpu.make_async_remote_copy(
            src_ref=src,
            dst_ref=dst,
            send_sem=send_sem,
            recv_sem=recv_sem,
            device_id=device,
            device_id_type=MESH,
        )

    def faces(g):
        return pl.ds(g * PART, PART)

    def half_of(ref, half, places):
        return ref.at[places, pl.ds(half * ROWS, ROWS)]

    def halo_hgt(half, row, g):
        return remote(
            half_of(master_hbm, half, faces(g)),
            windows[half].at[OWN, 1 - row, faces(g)],
            halo_h_send.at[half, row, g],
            halo_h_recv.at[half, 1 - row, g],
            beside[row],
        )

    def halo_partner(half):
        return remote(
            half_of(master_hbm, half, pl.ds(0, FACES)),
            windows[half].at[PARTNER, MID],
            halo_p_send.at[half],
            halo_p_recv.at[half],
            partner,
        )

    def halo_other(half, g):
        return remote(
            half_of(master_hbm, half, faces(g)),
            windows[half].at[OTHER, MID, faces(g)],
            halo_o_send.at[half, g],
            halo_o_recv.at[half, g],
            other,
        )

    def halo_turn(half, row):
        return remote(
            windows[half].at[OTHER, MID, faces(TURN)],
            windows[half].at[OTHER, 1 - row, faces(TURN)],
            halo_d_send.at[half, row],
            halo_d_recv.at[half, 1 - row],
            beside[row],
        )

    def halo_forward(half, column, row, g):
        return remote(
            windows[half].at[OWN, row, faces(g)],
            windows[half].at[column, row, faces(g)],
            halo_f_send.at[half, column - 1, row, g],
            halo_f_recv.at[half, column - 1, row, g],
            partner if column == PARTNER else other,
        )

    def force_len(half, column, g):
        if column == PARTNER:
            src, dst, device = send_p, recv_p, partner
        else:
            src, dst, device = send_o, recv_o, other
        return remote(
            src.at[half, g, pl.ds(0, 2)],
            dst.at[half, g, pl.ds(0, 2)],
            force_l_send.at[half, column - 1, g],
            force_l_recv.at[half, column - 1, g],
            device,
        )

    def force_mid(half, column, g):
        if column == PARTNER:
            src, dst, device = send_p, recv_p, partner
        else:
            src, dst, device = send_o, recv_o, other
        return remote(
            src.at[half, g, MID],
            dst.at[half, g, MID],
            force_m_send.at[half, column - 1, g],
            force_m_recv.at[half, column - 1, g],
            device,
        )

    def force_turn(half, row):
        return remote(
            send_o.at[half, TURN, row],
            recv_d.at[half, 1 - row],
            force_d_send.at[half, row],
            force_d_recv.at[half, 1 - row],
            beside[row],
        )

    def force_hgt(half, row, g):
        return remote(
            send_h.at[half, row, g],
            recv_h.at[half, 1 - row, g],
            force_h_send.at[half, row, g],
            force_h_recv.at[half, 1 - row, g],
            beside[row],
        )

    def to_other(action):
        pl.when(has_other)(action)

    def to_row(row, action):
        pl.when(has_row[row])(action)

    barrier = pltpu.get_barrier_semaphore()
    for device, there in neighbours:

        def greet(device=device):
            pl.semaphore_signal(barrier, inc=1, device_id=device, device_id_type=MESH)

        when(there, greet)
    loads = [
        pltpu.make_async_copy(coords, points, local_sem.at[0]),
        pltpu.make_async_copy(weights, point_weights, local_sem.at[1]),
        *[
            pltpu.make_async_copy(
                half_of(master_hbm, half, pl.ds(0, FACES)),
                windows[half].at[OWN, MID],
                local_sem.at[2 + half],
            )
            for half in range(HALVES)
        ],
        *[
            pltpu.make_async_copy(
                half_of(slave_hbm, half, pl.ds(0, FACES)), slave.at[half], local_sem.at[4 + half]
            )
            for half in range(HALVES)
        ],
    ]
    for load in loads:
        load.start()
    pl.semaphore_wait(barrier, 1 + sum(there.astype(jnp.int32) for _, there in neighbours[1:]))

    def send_own(half):
        @pl.when(has_other)
        def _():
            for g in (TURN, *range(TURN)):
                halo_other(half, g).start()

        halo_partner(half).start()
        for g in range(CHUNKS):
            for row in (DOWN, UP):
                to_row(row, lambda row=row, g=g: halo_hgt(half, row, g).start())

    send_own(0)
    order_pairs(pair_count, (slave_face, master_row, master_col, active), order)
    publish = pltpu.make_async_copy(order, meta, local_sem.at[6])
    publish.start()
    loads[0].wait()
    loads[1].wait()

    modes = lax.broadcasted_iota(jnp.int32, (ORDER, NODES), 0).astype(F32)
    row_ids = lax.broadcasted_iota(jnp.int32, (NODES, NODES), 0)
    col_ids = lax.broadcasted_iota(jnp.int32, (NODES, NODES), 1)

    def build_tables(first_pair):
        def one(i, _):
            place = points[first_pair + i]
            weight = point_weights[pl.ds(first_pair + i, 1), :]
            sx, sy, mx, my = (cos_pi(modes * place[k : k + 1]) for k in range(4))
            rows = pl.ds(pl.multiple_of((first_pair + i) * ORDER, ORDER), ORDER)
            tables[i, 0] = sx
            tables[i, 1] = sy
            tables[i, 2] = mx * weight
            tables[i, 3] = my
            first_sq[rows, :] = sx * sx * weight
            second_sq[rows, :] = sy * sy
            return 0

        lax.fori_loop(0, GROUP, one, 0)

    def build_dual():
        same_pair = row_ids // ORDER == col_ids // ORDER
        same_node = row_ids % ORDER == col_ids // ORDER
        spread = jnp.where(row_ids % ORDER == col_ids % ORDER, 1.0, 0.0).astype(BF16)
        spread = jnp.concatenate([spread, spread], axis=0)
        for k in range(PAIRS // GROUP):
            rows = pl.ds(k * GROUP * ORDER, GROUP * ORDER)
            high, low = split(first_sq[rows, :])
            left = jnp.concatenate([high, low, high], axis=1)
            high, low = split(second_sq[rows, :])
            right = jnp.concatenate([high, high, low], axis=1)
            sums = lax.dot_general(left, right, NT, preferred_element_type=F32)
            high, low = split(jnp.where(same_pair, sums, 0.0))
            wide = jnp.dot(
                jnp.concatenate([high, low], axis=1), spread, preferred_element_type=F32
            )
            wide = jnp.where(same_node, wide, 0.0)
            dual[k * GROUP : (k + 1) * GROUP, :] = jnp.sum(wide.reshape(GROUP, ORDER, NODES), axis=1)

    def table_of(i, k):
        first, second = tables[i, k], tables[i, k + 1]
        return (first[:, None, :] * second[None, :, :]).reshape(NODES, NODES)

    def build_mortar(first_pair):
        def some(step, _):
            for u in range(LOCK_A):
                i = step * LOCK_A + u
                slave_high, slave_low = split(table_of(i, 0))
                master_high, master_low = split(table_of(i, 2))
                left = jnp.concatenate([slave_high, slave_low, slave_high], axis=1)
                right = jnp.concatenate([master_high, master_high, master_low], axis=1)
                product = lax.dot_general(left, right, NT, preferred_element_type=F32)
                mortar[first_pair + i] = product.astype(BF16)
            return 0

        lax.fori_loop(0, GROUP // LOCK_A, some, 0)

    def relay(half, g):
        @pl.when((g == 0) & has_other)
        def _():
            halo_other(half, TURN).wait_recv()
            for row in (DOWN, UP):
                to_row(row, lambda row=row: halo_turn(half, row).start())

        for row in (DOWN, UP):

            def pass_on(row=row):
                halo_hgt(half, 1 - row, g).wait_recv()
                pl.when(has_other & (g != TURN))(lambda: halo_forward(half, OTHER, row, g).start())
                halo_forward(half, PARTNER, row, g).start()

            to_row(row, pass_on)

    def prepare(g, _):
        build_tables(g * GROUP)
        build_mortar(g * GROUP)
        relay(0, g)
        pl.when(g == CHUNKS - 2)(lambda: send_own(1))
        return 0

    lax.fori_loop(0, CHUNKS, prepare, 0)
    build_dual()

    @pl.when(jnp.logical_not(has_other))
    def _():
        recv_o[...] = jnp.zeros(recv_o.shape, BF16)

    for row in (DOWN, UP):

        @pl.when(jnp.logical_not(has_row[row]))
        def _(row=row):
            for half in range(HALVES):
                recv_h[half, row] = jnp.zeros(recv_h.shape[2:], BF16)
                recv_d[half, row] = jnp.zeros(recv_d.shape[2:], BF16)

    publish.wait()
    for load in loads[2:]:
        load.wait()

    def all_arrived(half):
        halo_partner(half).wait_recv()

        def arrived(g, _):
            pl.when(has_other & (g != TURN))(lambda: halo_other(half, g).wait_recv())
            for row in (DOWN, UP):

                def rest(row=row):
                    halo_forward(half, PARTNER, row, g).wait_recv()
                    pl.when(has_other & (g != TURN))(lambda: halo_forward(half, OTHER, row, g).wait_recv())
                    pl.when(has_other & (g == TURN))(lambda: halo_turn(half, 1 - row).wait_recv())

                to_row(row, rest)
            return 0

        lax.fori_loop(0, CHUNKS, arrived, 0)

    def contact(half, step):
        slots = [step * LOCK_B + u for u in range(LOCK_B)]
        pairs = [meta[AT_PAIR, t] for t in slots]
        keys = [meta[AT_MASTER, t] for t in slots]
        mortars = [mortar[p] for p in pairs]
        projected = []
        for key, matrix in zip(keys, mortars):
            spot = jnp.where(key < SPOTS, key, MID * FACES)
            block = spot // FACES
            master = windows[half][block // 3, block % 3, spot % FACES]
            projected.append(lax.dot_general(master, matrix, NT, preferred_element_type=F32))
        multipliers = []
        for t, p, key, part in zip(slots, pairs, keys, projected):
            diag = dual[pl.ds(p, 1), :]
            gap = slave[half, meta[AT_SLAVE, t]].astype(F32) * diag - part
            multipliers.append(jnp.where(key < SPOTS, gap * (1.0 / diag), 0.0))
        pushes = [
            jnp.dot(m.astype(BF16), matrix, preferred_element_type=F32)
            for m, matrix in zip(multipliers, mortars)
        ]
        for t, m in zip(slots, multipliers):
            mult[half, t] = m
        total = run[half, jnp.maximum(slots[0] - 1, 0)]
        last = meta[AT_MASTER, jnp.maximum(slots[0] - 1, 0)]
        for t, key, push in zip(slots, keys, pushes):
            total = jnp.where(key == last, total, 0.0) + push
            run[half, t] = total
            last = key

    def force(half, column, row, face):
        last = meta[AT_LAST, (column * 3 + row) * FACES + face]
        return jnp.where(last >= 0, run[half, jnp.maximum(last, 0)], 0.0)

    def fill(half, column, g, rows):
        send = send_p if column == PARTNER else send_o
        for row in rows:
            for i in range(PART):
                send[half, g, row, i] = force(half, column, row, g * PART + i).astype(send.dtype)

    def fill_all(half):
        def one(g, _):
            fill(half, OTHER, g, (DOWN, UP))
            fill(half, PARTNER, g, (DOWN, UP, MID))
            pl.when(g != TURN)(lambda: fill(half, OTHER, g, (MID,)))
            return 0

        lax.fori_loop(0, CHUNKS, one, 0)

    def send_all(half):
        for row in (DOWN, UP):
            to_row(row, lambda row=row: force_turn(half, row).start())

        @pl.when(has_other)
        def _():
            for g in range(TURN):
                force_len(half, OTHER, g).start()
            for g in range(TURN):
                force_mid(half, OTHER, g).start()

        for g in (TURN, *range(TURN)):
            force_len(half, PARTNER, g).start()
        for g in range(CHUNKS):
            force_mid(half, PARTNER, g).start()

    def add_slaves(half):
        slave_run[0] = jnp.zeros((ROWS, NODES), F32)

        def some(step, _):
            first = step * LOCK_S
            total = slave_run[jnp.maximum(first - 1, 0)]
            last = meta[AT_FACE, jnp.maximum(first - 1, 0)]
            for u in range(LOCK_S):
                face = meta[AT_FACE, first + u]
                total = jnp.where(face == last, total, 0.0) + mult[half, meta[AT_TURN, first + u]]
                slave_run[first + u] = total
                last = face
            return 0

        lax.fori_loop(0, PAIRS // LOCK_S, some, 0)

        def one(face, _):
            last = meta[AT_END, face]
            total = jnp.where(last >= 0, slave_run[jnp.maximum(last, 0)], 0.0)
            out_slave[face, half * ROWS : (half + 1) * ROWS, :] = total
            return 0

        lax.fori_loop(0, FACES, one, 0)

    def send_heights(half, k):
        g = lax.rem(k + TURN, CHUNKS)
        force_len(half, PARTNER, g).wait_recv()

        def own(row, i):
            return force(half, OWN, row, g * PART + i) + recv_p[half, g, row, i]

        @pl.when(g == TURN)
        def _():
            for row in (DOWN, UP):
                for i in range(PART):
                    send_h[half, row, g, i] = own(row, i).astype(BF16)

        @pl.when(g != TURN)
        def _():
            to_other(lambda: force_len(half, OTHER, g).wait_recv())
            for row in (DOWN, UP):
                for i in range(PART):
                    total = own(row, i) + recv_o[half, g, row, i].astype(F32)
                    send_h[half, row, g, i] = total.astype(BF16)

        for row in (DOWN, UP):
            to_row(row, lambda row=row: force_hgt(half, row, g).start())

        @pl.when(g == TURN)
        def _():
            for row in (DOWN, UP):
                to_row(row, lambda row=row: force_turn(half, 1 - row).wait_recv())
            for i in range(PART):
                total = force(half, OTHER, MID, g * PART + i)
                for row in (DOWN, UP):
                    total = total + recv_d[half, row, i].astype(F32)
                send_o[half, g, MID, i] = total.astype(BF16)
            to_other(lambda: force_mid(half, OTHER, g).start())

    def finish(half, g):
        force_mid(half, PARTNER, g).wait_recv()
        to_other(lambda: force_mid(half, OTHER, g).wait_recv())
        for row in (DOWN, UP):
            to_row(row, lambda row=row: force_hgt(half, 1 - row, g).wait_recv())
        for i in range(PART):
            total = force(half, OWN, MID, g * PART + i)
            total = total + recv_p[half, g, MID, i] + recv_o[half, g, MID, i].astype(F32)
            for row in (DOWN, UP):
                total = total + recv_h[half, row, g, i].astype(F32)
            out_master[g * PART + i, half * ROWS : (half + 1) * ROWS, :] = total

    for half in range(HALVES):
        run[half, 0] = jnp.zeros((ROWS, NODES), F32)

    all_arrived(0)

    def first_half(k, _):
        contact(0, k)
        pl.when(k % 2 == 0)(lambda: relay(1, k // 2))
        return 0

    lax.fori_loop(0, PAIRS // LOCK_B, first_half, 0)
    fill_all(0)
    relay(1, 2)
    send_all(0)
    relay(1, 3)

    all_arrived(1)

    def second_half(k, _):
        contact(1, k)
        send_heights(0, k)
        return 0

    lax.fori_loop(0, PAIRS // LOCK_B, second_half, 0)
    fill_all(1)
    send_all(1)
    for half in range(HALVES):
        add_slaves(half)

    def last_sums(k, _):
        send_heights(1, k)
        finish(0, k)
        return 0

    lax.fori_loop(0, CHUNKS, last_sums, 0)

    def last_faces(g, _):
        finish(1, g)
        return 0

    lax.fori_loop(0, CHUNKS, last_faces, 0)

    for half in range(HALVES):
        halo_partner(half).wait_send()
        for row in (DOWN, UP):
            to_row(row, lambda row=row, half=half: force_turn(half, row).wait_send())
            pl.when(has_row[row] & has_other)(
                lambda row=row, half=half: halo_turn(half, row).wait_send()
            )

        def sent(g, _, half=half):
            to_other(lambda: halo_other(half, g).wait_send())
            force_len(half, PARTNER, g).wait_send()
            force_mid(half, PARTNER, g).wait_send()
            to_other(lambda: force_mid(half, OTHER, g).wait_send())
            pl.when(has_other & (g != TURN))(lambda: force_len(half, OTHER, g).wait_send())
            for row in (DOWN, UP):

                def rest(row=row):
                    halo_hgt(half, row, g).wait_send()
                    force_hgt(half, row, g).wait_send()
                    halo_forward(half, PARTNER, row, g).wait_send()
                    pl.when(has_other & (g != TURN))(lambda: halo_forward(half, OTHER, row, g).wait_send())

                to_row(row, rest)
            return 0

        lax.fori_loop(0, CHUNKS, sent, 0)


def store(master_in, slave_in, master_out, slave_out, sem):
    copies = [
        pltpu.make_async_copy(master_in, master_out, sem.at[0]),
        pltpu.make_async_copy(slave_in, slave_out, sem.at[1]),
    ]
    for copy in copies:
        copy.start()
    for copy in copies:
        copy.wait()


def body(
    slave_disp,
    master_disp,
    quad_coords,
    quad_weights,
    pair_count,
    slave_face,
    master_row,
    master_col,
    active,
):
    face = (CHANNELS, NODES)
    dma = pltpu.SemaphoreType.DMA
    out = jax.ShapeDtypeStruct((FACES, *face), F32)
    held = pltpu.VMEM((FACES, *face), F32)
    vmem = pl.BlockSpec(memory_space=pltpu.VMEM)
    hbm = pl.BlockSpec(memory_space=pl.ANY)
    slots = (1, PAIRS)
    part = (ROWS, NODES)
    results = pl.pallas_call(
        kernel,
        out_shape=(held, held),
        in_specs=[pl.BlockSpec(memory_space=pltpu.SMEM), *[vmem] * 4, *[hbm] * 4],
        out_specs=(vmem, vmem),
        scratch_shapes=[
            pltpu.VMEM(META, jnp.int32),
            pltpu.SMEM(META, jnp.int32),
            pltpu.VMEM((PAIRS, 4, NODES), F32),
            pltpu.VMEM((PAIRS, NODES), F32),
            *[pltpu.VMEM((3, 3, FACES, *part), BF16)] * HALVES,
            pltpu.VMEM((HALVES, FACES, *part), BF16),
            pltpu.VMEM((PAIRS, NODES, NODES), BF16),
            pltpu.VMEM((PAIRS, NODES), F32),
            pltpu.VMEM((GROUP, 4, ORDER, NODES), F32),
            pltpu.VMEM((PAIRS * ORDER, NODES), F32),
            pltpu.VMEM((PAIRS * ORDER, NODES), F32),
            pltpu.VMEM((HALVES, PAIRS, *part), F32),
            pltpu.VMEM((HALVES, PAIRS, *part), F32),
            pltpu.VMEM((PAIRS, *part), F32),
            pltpu.VMEM((HALVES, CHUNKS, 3, PART, *part), F32),
            pltpu.VMEM((HALVES, CHUNKS, 3, PART, *part), F32),
            pltpu.VMEM((HALVES, CHUNKS, 3, PART, *part), BF16),
            pltpu.VMEM((HALVES, CHUNKS, 3, PART, *part), BF16),
            pltpu.VMEM((HALVES, 2, PART, *part), BF16),
            pltpu.VMEM((HALVES, 2, CHUNKS, PART, *part), BF16),
            pltpu.VMEM((HALVES, 2, CHUNKS, PART, *part), BF16),
            dma((7,)),
            *[dma((HALVES, 2, CHUNKS))] * 2,
            *[dma((HALVES,))] * 2,
            *[dma((HALVES, CHUNKS))] * 2,
            *[dma((HALVES, 2))] * 2,
            *[dma((HALVES, 2, 2, CHUNKS))] * 2,
            *[dma((HALVES, 2, CHUNKS))] * 2,
            *[dma((HALVES, 2, CHUNKS))] * 2,
            *[dma((HALVES, 2))] * 2,
            *[dma((HALVES, 2, CHUNKS))] * 2,
        ],
        compiler_params=pltpu.CompilerParams(
            collective_id=0, has_side_effects=True, vmem_limit_bytes=57 * 2**20
        ),
        name="contact",
    )(
        pair_count,
        slave_face.reshape(slots),
        master_row.reshape(slots),
        master_col.reshape(slots),
        active.reshape(slots),
        quad_coords.reshape(PAIRS, 4, NODES),
        quad_weights.reshape(PAIRS, NODES),
        slave_disp.reshape(FACES, *face),
        master_disp.reshape(FACES, *face),
    )
    results = [pltpu.with_memory_space_constraint(r, pltpu.VMEM) for r in results]
    master_force, slave_sum = pl.pallas_call(
        store,
        out_shape=(out, out),
        in_specs=[vmem, vmem],
        out_specs=(hbm, hbm),
        scratch_shapes=[dma((2,))],
        compiler_params=pltpu.CompilerParams(vmem_limit_bytes=2**20),
        name="store",
    )(*results)
    return (
        master_force.reshape(4, 4, *face),
        slave_sum.reshape(4, 4, *face),
    )


def solution(mesh):
    in_specs = (
        P("len", "hgt", None, None),
        P("len", "hgt", None, None),
        P("len", "hgt", None, None, None),
        P("len", "hgt", None, None),
        P("len", "hgt"),
        P("len", "hgt", None),
        P("len", "hgt", None),
        P("len", "hgt", None),
        P("len", "hgt", None),
    )
    out_specs = (P("len", "hgt", None, None), P("len", "hgt", None, None))
    return jax.shard_map(body, mesh=mesh, in_specs=in_specs, out_specs=out_specs, check_vma=False)
```

```python
import functools

import jax
import jax.numpy as jnp
from jax import lax
from jax.experimental import pallas as pl
from jax.experimental.pallas import tpu as pltpu
from jax.sharding import PartitionSpec as P

ORDER = 16
NODES = 256
CHANNELS = 96
FACES = 16
PAIRS = 64
GROUP = 8
SQUARES = 16
LOCK_A = 8
LOCK_S = 8
LOCK_B = 16
CHUNKS = 4
HALVES = 2
ROWS = CHANNELS // HALVES
PART = FACES // CHUNKS
F32, BF16 = jnp.float32, jnp.bfloat16
MESH = pl.DeviceIdType.MESH
NT = (((1,), (1,)), ((), ()))
NN = (((1,), (0,)), ((), ()))

OWN, PARTNER, OTHER = range(3)
DOWN, UP, MID = range(3)
BLOCKS = 9
SPOTS = BLOCKS * FACES

AT_PAIR, AT_MASTER, AT_SLAVE, AT_LAST = range(4)
AT_TURN, AT_FACE, AT_END = range(4, 7)
META = (8, 256)
TURN = CHUNKS - 1


def cos_pi(turns):
    reduced = turns - 2.0 * jnp.round(turns * 0.5)
    s = (0.5 - jnp.abs(reduced)) - 1.4e-8
    s2 = s * s
    p = jnp.float32(-0.00737043)
    for c in (0.082145887, -0.59926453, 2.5501640, -5.1677128, 3.1415927):
        p = p * s2 + jnp.float32(c)
    return p * s


def split(value):
    high = value.astype(BF16)
    return high, (value - high.astype(F32)).astype(BF16)


def order_pairs(pair_count, ints, order):
    side = 4
    at_len, at_hgt = lax.axis_index("len"), lax.axis_index("hgt")
    square = (PAIRS, PAIRS)
    down, along = (lax.broadcasted_iota(jnp.int32, square, d) for d in (0, 1))
    slots = lax.broadcasted_iota(jnp.int32, (1, PAIRS), 1)
    slave_face, master_row, master_col, active = (ref[...] for ref in ints)
    live = (slots < pair_count[0, 0]) & (active == 1)
    step_len = master_row // side - at_len
    step_hgt = master_col // side - at_hgt
    column = jnp.where(step_len == 0, OWN, jnp.where(step_len == 1 - 2 * lax.rem(at_len, 2), PARTNER, OTHER))
    row = jnp.where(step_hgt == 0, MID, jnp.where(step_hgt < 0, DOWN, UP))
    spot = (column * 3 + row) * FACES + (master_row % side) * side + master_col % side
    key = jnp.where(live, spot, SPOTS)

    def stand(values):
        return jnp.sum(jnp.where(down == along, values, 0), axis=1, keepdims=True)

    def rank_of(key, key_col):
        before = (key < key_col) | ((key == key_col) & (along < down))
        return jnp.sum(before.astype(jnp.int32), axis=1, keepdims=True)

    def pick(rank, values):
        return jnp.sum(jnp.where(rank == along, values, 0), axis=0, keepdims=True)

    spots = lax.broadcasted_iota(jnp.int32, (PAIRS, META[1]), 1)

    def last_of(key_col):
        has = jnp.sum((key_col == spots).astype(jnp.int32), axis=0, keepdims=True)
        upto = jnp.sum((key_col <= spots).astype(jnp.int32), axis=0, keepdims=True)
        return jnp.where(has > 0, upto - 1, -1)

    key_col = stand(key)
    rank = rank_of(key, key_col)
    face_key = jnp.where(live, slave_face, FACES)
    face_col = stand(face_key)
    face_rank = rank_of(face_key, face_col)
    order[...] = jnp.zeros(META, jnp.int32)
    order[AT_PAIR : AT_PAIR + 1, :PAIRS] = pick(rank, down)
    order[AT_MASTER : AT_MASTER + 1, :PAIRS] = pick(rank, key_col)
    order[AT_SLAVE : AT_SLAVE + 1, :PAIRS] = pick(rank, stand(slave_face))
    order[AT_LAST : AT_LAST + 1, :] = last_of(key_col)
    order[AT_TURN : AT_TURN + 1, :PAIRS] = pick(face_rank, rank)
    order[AT_FACE : AT_FACE + 1, :PAIRS] = pick(face_rank, face_col)
    order[AT_END : AT_END + 1, :] = last_of(face_col)


def kernel(
    pair_count,
    slave_face,
    master_row,
    master_col,
    active,
    coords,
    weights,
    slave_hbm,
    master_hbm,
    out_master,
    out_slave,
    order,
    meta,
    points,
    point_weights,
    window_first,
    window_second,
    slave,
    mortar,
    dual,
    tables,
    first_sq,
    second_sq,
    run,
    mult,
    slave_run,
    send_p,
    recv_p,
    send_o,
    recv_o,
    recv_d,
    send_h,
    recv_h,
    local_sem,
    halo_h_send,
    halo_h_recv,
    halo_p_send,
    halo_p_recv,
    halo_o_send,
    halo_o_recv,
    halo_d_send,
    halo_d_recv,
    halo_f_send,
    halo_f_recv,
    force_l_send,
    force_l_recv,
    force_m_send,
    force_m_recv,
    force_d_send,
    force_d_recv,
    force_h_send,
    force_h_recv,
):
    windows = (window_first, window_second)
    at_len = lax.axis_index("len")
    at_hgt = lax.axis_index("hgt")
    n_len = lax.axis_size("len")
    n_hgt = lax.axis_size("hgt")
    odd = lax.rem(at_len, 2)
    other_len = at_len - 1 + 2 * odd
    partner = (at_len + 1 - 2 * odd, at_hgt)
    other = (lax.rem(other_len + n_len, n_len), at_hgt)
    above = (at_len, lax.rem(at_hgt + 1, n_hgt))
    below = (at_len, lax.rem(at_hgt + n_hgt - 1, n_hgt))
    has_other = (other_len >= 0) & (other_len < n_len)
    has_row = (at_hgt > 0, at_hgt < n_hgt - 1)
    beside = (below, above)
    neighbours = ((partner, None), (other, has_other), (below, has_row[DOWN]), (above, has_row[UP]))

    def when(condition, action):
        if condition is None:
            action()
        else:
            pl.when(condition)(action)

    def remote(src, dst, send_sem, recv_sem, device):
        return pltpu.make_async_remote_copy(
            src_ref=src,
            dst_ref=dst,
            send_sem=send_sem,
            recv_sem=recv_sem,
            device_id=device,
            device_id_type=MESH,
        )

    def faces(g):
        return pl.ds(g * PART, PART)

    def half_of(ref, half, places):
        return ref.at[places, pl.ds(half * ROWS, ROWS)]

    def halo_hgt(half, row, g):
        return remote(
            half_of(master_hbm, half, faces(g)),
            windows[half].at[OWN, 1 - row, faces(g)],
            halo_h_send.at[half, row, g],
            halo_h_recv.at[half, 1 - row, g],
            beside[row],
        )

    def halo_partner(half):
        return remote(
            half_of(master_hbm, half, pl.ds(0, FACES)),
            windows[half].at[PARTNER, MID],
            halo_p_send.at[half],
            halo_p_recv.at[half],
            partner,
        )

    def halo_other(half, g):
        return remote(
            half_of(master_hbm, half, faces(g)),
            windows[half].at[OTHER, MID, faces(g)],
            halo_o_send.at[half, g],
            halo_o_recv.at[half, g],
            other,
        )

    def halo_turn(half, row):
        return remote(
            windows[half].at[OTHER, MID, faces(TURN)],
            windows[half].at[OTHER, 1 - row, faces(TURN)],
            halo_d_send.at[half, row],
            halo_d_recv.at[half, 1 - row],
            beside[row],
        )

    def halo_forward(half, column, row, g):
        return remote(
            windows[half].at[OWN, row, faces(g)],
            windows[half].at[column, row, faces(g)],
            halo_f_send.at[half, column - 1, row, g],
            halo_f_recv.at[half, column - 1, row, g],
            partner if column == PARTNER else other,
        )

    def force_len(half, column, g):
        if column == PARTNER:
            src, dst, device = send_p, recv_p, partner
        else:
            src, dst, device = send_o, recv_o, other
        return remote(
            src.at[half, g, pl.ds(0, 2)],
            dst.at[half, g, pl.ds(0, 2)],
            force_l_send.at[half, column - 1, g],
            force_l_recv.at[half, column - 1, g],
            device,
        )

    def force_mid(half, column, g):
        if column == PARTNER:
            src, dst, device = send_p, recv_p, partner
        else:
            src, dst, device = send_o, recv_o, other
        return remote(
            src.at[half, g, MID],
            dst.at[half, g, MID],
            force_m_send.at[half, column - 1, g],
            force_m_recv.at[half, column - 1, g],
            device,
        )

    def force_turn(half, row):
        return remote(
            send_o.at[half, TURN, row],
            recv_d.at[half, 1 - row],
            force_d_send.at[half, row],
            force_d_recv.at[half, 1 - row],
            beside[row],
        )

    def force_hgt(half, row, g):
        return remote(
            send_h.at[half, row, g],
            recv_h.at[half, 1 - row, g],
            force_h_send.at[half, row, g],
            force_h_recv.at[half, 1 - row, g],
            beside[row],
        )

    def to_other(action):
        pl.when(has_other)(action)

    def to_row(row, action):
        pl.when(has_row[row])(action)

    barrier = pltpu.get_barrier_semaphore()
    for device, there in neighbours:

        def greet(device=device):
            pl.semaphore_signal(barrier, inc=1, device_id=device, device_id_type=MESH)

        when(there, greet)
    loads = [
        pltpu.make_async_copy(coords, points, local_sem.at[0]),
        pltpu.make_async_copy(weights, point_weights, local_sem.at[1]),
        *[
            pltpu.make_async_copy(
                half_of(master_hbm, half, pl.ds(0, FACES)),
                windows[half].at[OWN, MID],
                local_sem.at[2 + half],
            )
            for half in range(HALVES)
        ],
        *[
            pltpu.make_async_copy(
                half_of(slave_hbm, half, pl.ds(0, FACES)), slave.at[half], local_sem.at[4 + half]
            )
            for half in range(HALVES)
        ],
    ]
    for load in loads:
        load.start()
    pl.semaphore_wait(barrier, 1 + sum(there.astype(jnp.int32) for _, there in neighbours[1:]))

    def send_own(half):
        @pl.when(has_other)
        def _():
            for g in (TURN, *range(TURN)):
                halo_other(half, g).start()

        halo_partner(half).start()
        for g in range(CHUNKS):
            for row in (DOWN, UP):
                to_row(row, lambda row=row, g=g: halo_hgt(half, row, g).start())

    send_own(0)
    order_pairs(pair_count, (slave_face, master_row, master_col, active), order)
    publish = pltpu.make_async_copy(order, meta, local_sem.at[6])
    publish.start()
    loads[0].wait()
    loads[1].wait()

    modes = lax.broadcasted_iota(jnp.int32, (ORDER, NODES), 0).astype(F32)
    row_ids = lax.broadcasted_iota(jnp.int32, (NODES, NODES), 0)
    col_ids = lax.broadcasted_iota(jnp.int32, (NODES, NODES), 1)

    def build_tables(first_pair):
        def one(i, _):
            place = points[first_pair + i]
            weight = point_weights[pl.ds(first_pair + i, 1), :]
            sx, sy, mx, my = (cos_pi(modes * place[k : k + 1]) for k in range(4))
            rows = pl.ds(pl.multiple_of((first_pair + i) * ORDER, ORDER), ORDER)
            tables[i, 0] = sx
            tables[i, 1] = sy
            tables[i, 2] = mx * weight
            tables[i, 3] = my
            first_sq[rows, :] = sx * sx * weight
            second_sq[rows, :] = sy * sy
            return 0

        lax.fori_loop(0, GROUP, one, 0)

    def build_dual():
        same_pair = row_ids // ORDER == col_ids // ORDER
        same_node = row_ids % ORDER == col_ids // ORDER
        spread = jnp.where(row_ids % ORDER == col_ids % ORDER, 1.0, 0.0).astype(BF16)
        spread = jnp.concatenate([spread, spread], axis=0)
        for k in range(PAIRS // SQUARES):
            rows = pl.ds(k * SQUARES * ORDER, SQUARES * ORDER)
            high, low = split(first_sq[rows, :])
            left = jnp.concatenate([high, low, high], axis=1)
            high, low = split(second_sq[rows, :])
            right = jnp.concatenate([high, high, low], axis=1)
            sums = lax.dot_general(left, right, NT, preferred_element_type=F32)
            high, low = split(jnp.where(same_pair, sums, 0.0))
            wide = jnp.dot(
                jnp.concatenate([high, low], axis=1), spread, preferred_element_type=F32
            )
            wide = jnp.where(same_node, wide, 0.0)
            dual[k * SQUARES : (k + 1) * SQUARES, :] = jnp.sum(wide.reshape(SQUARES, ORDER, NODES), axis=1)

    def table_of(i, k):
        first, second = tables[i, k], tables[i, k + 1]
        return (first[:, None, :] * second[None, :, :]).reshape(NODES, NODES)

    def build_mortar(first_pair):
        def some(step, _):
            for u in range(LOCK_A):
                i = step * LOCK_A + u
                slave_high, slave_low = split(table_of(i, 0))
                master_high, master_low = split(table_of(i, 2))
                left = jnp.concatenate([slave_high, slave_low, slave_high], axis=1)
                right = jnp.concatenate([master_high, master_high, master_low], axis=1)
                product = lax.dot_general(left, right, NT, preferred_element_type=F32)
                mortar[first_pair + i] = product.astype(BF16)
            return 0

        lax.fori_loop(0, GROUP // LOCK_A, some, 0)

    def relay(half, g):
        @pl.when((g == 0) & has_other)
        def _():
            halo_other(half, TURN).wait_recv()
            for row in (DOWN, UP):
                to_row(row, lambda row=row: halo_turn(half, row).start())

        for row in (DOWN, UP):

            def pass_on(row=row):
                halo_hgt(half, 1 - row, g).wait_recv()
                pl.when(has_other & (g != TURN))(lambda: halo_forward(half, OTHER, row, g).start())
                halo_forward(half, PARTNER, row, g).start()

            to_row(row, pass_on)

    def prepare(g, _):
        build_tables(g * GROUP)
        build_mortar(g * GROUP)
        for at, chunk in ((1, 0), (4, 2)):
            pl.when((g == at) | (g == at + 1))(lambda: relay(0, chunk + g - at))
        pl.when(g == 4)(lambda: send_own(1))
        return 0

    lax.fori_loop(0, PAIRS // GROUP, prepare, 0)
    build_dual()

    @pl.when(jnp.logical_not(has_other))
    def _():
        recv_o[...] = jnp.zeros(recv_o.shape, BF16)

    for row in (DOWN, UP):

        @pl.when(jnp.logical_not(has_row[row]))
        def _(row=row):
            for half in range(HALVES):
                recv_h[half, row] = jnp.zeros(recv_h.shape[2:], BF16)
                recv_d[half, row] = jnp.zeros(recv_d.shape[2:], BF16)

    publish.wait()
    for load in loads[2:]:
        load.wait()

    def all_arrived(half):
        halo_partner(half).wait_recv()

        def arrived(g, _):
            pl.when(has_other & (g != TURN))(lambda: halo_other(half, g).wait_recv())
            for row in (DOWN, UP):

                def rest(row=row):
                    halo_forward(half, PARTNER, row, g).wait_recv()
                    pl.when(has_other & (g != TURN))(lambda: halo_forward(half, OTHER, row, g).wait_recv())
                    pl.when(has_other & (g == TURN))(lambda: halo_turn(half, 1 - row).wait_recv())

                to_row(row, rest)
            return 0

        lax.fori_loop(0, CHUNKS, arrived, 0)

    def contact(half, step):
        slots = [step * LOCK_B + u for u in range(LOCK_B)]
        pairs = [meta[AT_PAIR, t] for t in slots]
        keys = [meta[AT_MASTER, t] for t in slots]
        mortars = [mortar[p] for p in pairs]
        projected = []
        for key, matrix in zip(keys, mortars):
            spot = jnp.where(key < SPOTS, key, MID * FACES)
            block = spot // FACES
            master = windows[half][block // 3, block % 3, spot % FACES]
            projected.append(lax.dot_general(master, matrix, NT, preferred_element_type=F32))
        multipliers = []
        for t, p, key, part in zip(slots, pairs, keys, projected):
            diag = dual[pl.ds(p, 1), :]
            gap = slave[half, meta[AT_SLAVE, t]].astype(F32) * diag - part
            multipliers.append(jnp.where(key < SPOTS, gap * (1.0 / diag), 0.0))
        pushes = [
            jnp.dot(m.astype(BF16), matrix, preferred_element_type=F32)
            for m, matrix in zip(multipliers, mortars)
        ]
        for t, m in zip(slots, multipliers):
            mult[half, t] = m
        total = run[half, jnp.maximum(slots[0] - 1, 0)]
        last = meta[AT_MASTER, jnp.maximum(slots[0] - 1, 0)]
        for t, key, push in zip(slots, keys, pushes):
            total = jnp.where(key == last, total, 0.0) + push
            run[half, t] = total
            last = key

    def force(half, column, row, face):
        last = meta[AT_LAST, (column * 3 + row) * FACES + face]
        return jnp.where(last >= 0, run[half, jnp.maximum(last, 0)], 0.0)

    def fill(half, column, g, rows):
        send = send_p if column == PARTNER else send_o
        for row in rows:
            for i in range(PART):
                send[half, g, row, i] = force(half, column, row, g * PART + i).astype(send.dtype)

    def send_all(half):
        def side(k, _):
            g = lax.rem(k + TURN, CHUNKS)
            fill(half, OTHER, g, (DOWN, UP))

            @pl.when(g == TURN)
            def _():
                for row in (DOWN, UP):
                    to_row(row, lambda row=row: force_turn(half, row).start())

            pl.when(has_other & (g != TURN))(lambda: force_len(half, OTHER, g).start())
            return 0

        def partner_side(k, _):
            g = lax.rem(k + TURN, CHUNKS)
            fill(half, PARTNER, g, (DOWN, UP))
            force_len(half, PARTNER, g).start()
            return 0

        def middle(g, _):
            fill(half, OTHER, g, (MID,))
            to_other(lambda: force_mid(half, OTHER, g).start())
            return 0

        def partner_middle(g, _):
            fill(half, PARTNER, g, (MID,))
            force_mid(half, PARTNER, g).start()
            return 0

        lax.fori_loop(0, CHUNKS, side, 0)
        lax.fori_loop(0, CHUNKS, partner_side, 0)
        lax.fori_loop(0, TURN, middle, 0)
        lax.fori_loop(0, CHUNKS, partner_middle, 0)

    def add_slaves(half):
        slave_run[0] = jnp.zeros((ROWS, NODES), F32)

        def some(step, _):
            first = step * LOCK_S
            total = slave_run[jnp.maximum(first - 1, 0)]
            last = meta[AT_FACE, jnp.maximum(first - 1, 0)]
            for u in range(LOCK_S):
                face = meta[AT_FACE, first + u]
                total = jnp.where(face == last, total, 0.0) + mult[half, meta[AT_TURN, first + u]]
                slave_run[first + u] = total
                last = face
            return 0

        lax.fori_loop(0, PAIRS // LOCK_S, some, 0)

        def one(face, _):
            last = meta[AT_END, face]
            total = jnp.where(last >= 0, slave_run[jnp.maximum(last, 0)], 0.0)
            out_slave[face, half * ROWS : (half + 1) * ROWS, :] = total
            return 0

        lax.fori_loop(0, FACES, one, 0)

    def send_heights(half, k):
        g = lax.rem(k + TURN, CHUNKS)
        force_len(half, PARTNER, g).wait_recv()

        def own(row, i):
            return force(half, OWN, row, g * PART + i) + recv_p[half, g, row, i]

        @pl.when(g == TURN)
        def _():
            for row in (DOWN, UP):
                for i in range(PART):
                    send_h[half, row, g, i] = own(row, i).astype(BF16)

        @pl.when(g != TURN)
        def _():
            to_other(lambda: force_len(half, OTHER, g).wait_recv())
            for row in (DOWN, UP):
                for i in range(PART):
                    total = own(row, i) + recv_o[half, g, row, i].astype(F32)
                    send_h[half, row, g, i] = total.astype(BF16)

        for row in (DOWN, UP):
            to_row(row, lambda row=row: force_hgt(half, row, g).start())

    def send_turned(half):
        for row in (DOWN, UP):
            to_row(row, lambda row=row: force_turn(half, 1 - row).wait_recv())
        for i in range(PART):
            total = force(half, OTHER, MID, TURN * PART + i)
            for row in (DOWN, UP):
                total = total + recv_d[half, row, i].astype(F32)
            send_o[half, TURN, MID, i] = total.astype(BF16)
        to_other(lambda: force_mid(half, OTHER, TURN).start())

    def finish(half, g):
        force_mid(half, PARTNER, g).wait_recv()
        to_other(lambda: force_mid(half, OTHER, g).wait_recv())
        for row in (DOWN, UP):
            to_row(row, lambda row=row: force_hgt(half, 1 - row, g).wait_recv())
        for i in range(PART):
            total = force(half, OWN, MID, g * PART + i)
            total = total + recv_p[half, g, MID, i] + recv_o[half, g, MID, i].astype(F32)
            for row in (DOWN, UP):
                total = total + recv_h[half, row, g, i].astype(F32)
            out_master[g * PART + i, half * ROWS : (half + 1) * ROWS, :] = total

    for half in range(HALVES):
        run[half, 0] = jnp.zeros((ROWS, NODES), F32)

    all_arrived(0)
    relay(1, 0)

    def first_half(k, _):
        contact(0, k)
        pl.when(k % 2 == 0)(lambda: relay(1, k // 2 + 1))
        return 0

    lax.fori_loop(0, PAIRS // LOCK_B, first_half, 0)
    send_all(0)
    relay(1, 3)

    all_arrived(1)

    def second_half(k, _):
        contact(1, k)
        send_heights(0, k)
        return 0

    lax.fori_loop(0, PAIRS // LOCK_B, second_half, 0)
    send_turned(0)
    send_all(1)
    for half in range(HALVES):
        add_slaves(half)

    def last_sums(k, _):
        send_heights(1, k)
        pl.when(k == 2)(lambda: send_turned(1))
        finish(0, k)
        return 0

    lax.fori_loop(0, CHUNKS, last_sums, 0)

    def last_faces(g, _):
        finish(1, g)
        return 0

    lax.fori_loop(0, CHUNKS, last_faces, 0)

    for half in range(HALVES):
        halo_partner(half).wait_send()
        for row in (DOWN, UP):
            to_row(row, lambda row=row, half=half: force_turn(half, row).wait_send())
            pl.when(has_row[row] & has_other)(
                lambda row=row, half=half: halo_turn(half, row).wait_send()
            )

        def sent(g, _, half=half):
            to_other(lambda: halo_other(half, g).wait_send())
            force_len(half, PARTNER, g).wait_send()
            force_mid(half, PARTNER, g).wait_send()
            to_other(lambda: force_mid(half, OTHER, g).wait_send())
            pl.when(has_other & (g != TURN))(lambda: force_len(half, OTHER, g).wait_send())
            for row in (DOWN, UP):

                def rest(row=row):
                    halo_hgt(half, row, g).wait_send()
                    force_hgt(half, row, g).wait_send()
                    halo_forward(half, PARTNER, row, g).wait_send()
                    pl.when(has_other & (g != TURN))(lambda: halo_forward(half, OTHER, row, g).wait_send())

                to_row(row, rest)
            return 0

        lax.fori_loop(0, CHUNKS, sent, 0)


def store(master_in, slave_in, master_out, slave_out, sem):
    copies = [
        pltpu.make_async_copy(master_in, master_out, sem.at[0]),
        pltpu.make_async_copy(slave_in, slave_out, sem.at[1]),
    ]
    for copy in copies:
        copy.start()
    for copy in copies:
        copy.wait()


def body(
    slave_disp,
    master_disp,
    quad_coords,
    quad_weights,
    pair_count,
    slave_face,
    master_row,
    master_col,
    active,
):
    face = (CHANNELS, NODES)
    dma = pltpu.SemaphoreType.DMA
    out = jax.ShapeDtypeStruct((FACES, *face), F32)
    held = pltpu.VMEM((FACES, *face), F32)
    vmem = pl.BlockSpec(memory_space=pltpu.VMEM)
    hbm = pl.BlockSpec(memory_space=pl.ANY)
    slots = (1, PAIRS)
    part = (ROWS, NODES)
    results = pl.pallas_call(
        kernel,
        out_shape=(held, held),
        in_specs=[pl.BlockSpec(memory_space=pltpu.SMEM), *[vmem] * 4, *[hbm] * 4],
        out_specs=(vmem, vmem),
        scratch_shapes=[
            pltpu.VMEM(META, jnp.int32),
            pltpu.SMEM(META, jnp.int32),
            pltpu.VMEM((PAIRS, 4, NODES), F32),
            pltpu.VMEM((PAIRS, NODES), F32),
            *[pltpu.VMEM((3, 3, FACES, *part), BF16)] * HALVES,
            pltpu.VMEM((HALVES, FACES, *part), BF16),
            pltpu.VMEM((PAIRS, NODES, NODES), BF16),
            pltpu.VMEM((PAIRS, NODES), F32),
            pltpu.VMEM((GROUP, 4, ORDER, NODES), F32),
            pltpu.VMEM((PAIRS * ORDER, NODES), F32),
            pltpu.VMEM((PAIRS * ORDER, NODES), F32),
            pltpu.VMEM((HALVES, PAIRS, *part), F32),
            pltpu.VMEM((HALVES, PAIRS, *part), F32),
            pltpu.VMEM((PAIRS, *part), F32),
            pltpu.VMEM((HALVES, CHUNKS, 3, PART, *part), F32),
            pltpu.VMEM((HALVES, CHUNKS, 3, PART, *part), F32),
            pltpu.VMEM((HALVES, CHUNKS, 3, PART, *part), BF16),
            pltpu.VMEM((HALVES, CHUNKS, 3, PART, *part), BF16),
            pltpu.VMEM((HALVES, 2, PART, *part), BF16),
            pltpu.VMEM((HALVES, 2, CHUNKS, PART, *part), BF16),
            pltpu.VMEM((HALVES, 2, CHUNKS, PART, *part), BF16),
            dma((7,)),
            *[dma((HALVES, 2, CHUNKS))] * 2,
            *[dma((HALVES,))] * 2,
            *[dma((HALVES, CHUNKS))] * 2,
            *[dma((HALVES, 2))] * 2,
            *[dma((HALVES, 2, 2, CHUNKS))] * 2,
            *[dma((HALVES, 2, CHUNKS))] * 2,
            *[dma((HALVES, 2, CHUNKS))] * 2,
            *[dma((HALVES, 2))] * 2,
            *[dma((HALVES, 2, CHUNKS))] * 2,
        ],
        compiler_params=pltpu.CompilerParams(
            collective_id=0, has_side_effects=True, vmem_limit_bytes=57 * 2**20
        ),
        name="contact",
    )(
        pair_count,
        slave_face.reshape(slots),
        master_row.reshape(slots),
        master_col.reshape(slots),
        active.reshape(slots),
        quad_coords.reshape(PAIRS, 4, NODES),
        quad_weights.reshape(PAIRS, NODES),
        slave_disp.reshape(FACES, *face),
        master_disp.reshape(FACES, *face),
    )
    results = [pltpu.with_memory_space_constraint(r, pltpu.VMEM) for r in results]
    master_force, slave_sum = pl.pallas_call(
        store,
        out_shape=(out, out),
        in_specs=[vmem, vmem],
        out_specs=(hbm, hbm),
        scratch_shapes=[dma((2,))],
        compiler_params=pltpu.CompilerParams(vmem_limit_bytes=2**20),
        name="store",
    )(*results)
    return (
        master_force.reshape(4, 4, *face),
        slave_sum.reshape(4, 4, *face),
    )


def solution(mesh):
    in_specs = (
        P("len", "hgt", None, None),
        P("len", "hgt", None, None),
        P("len", "hgt", None, None, None),
        P("len", "hgt", None, None),
        P("len", "hgt"),
        P("len", "hgt", None),
        P("len", "hgt", None),
        P("len", "hgt", None),
        P("len", "hgt", None),
    )
    out_specs = (P("len", "hgt", None, None), P("len", "hgt", None, None))
    return jax.shard_map(body, mesh=mesh, in_specs=in_specs, out_specs=out_specs, check_vma=False)
```

```python
import functools

import jax
import jax.numpy as jnp
from jax import lax
from jax.experimental import pallas as pl
from jax.experimental.pallas import tpu as pltpu
from jax.sharding import PartitionSpec as P

ORDER = 16
NODES = 256
CHANNELS = 96
FACES = 16
PAIRS = 64
GROUP = 8
SQUARES = 16
LOCK_A = 8
LOCK_S = 8
LOCK_B = 16
CHUNKS = 4
HALVES = 2
ROWS = CHANNELS // HALVES
PART = FACES // CHUNKS
F32, BF16 = jnp.float32, jnp.bfloat16
MESH = pl.DeviceIdType.MESH
NT = (((1,), (1,)), ((), ()))
NN = (((1,), (0,)), ((), ()))

OWN, PARTNER, OTHER = range(3)
DOWN, UP, MID = range(3)
BLOCKS = 9
SPOTS = BLOCKS * FACES

AT_PAIR, AT_MASTER, AT_SLAVE, AT_LAST = range(4)
AT_TURN, AT_FACE, AT_END = range(4, 7)
META = (8, 256)
TURN = CHUNKS - 1


def cos_pi(turns):
    reduced = turns - 2.0 * jnp.round(turns * 0.5)
    s = (0.5 - jnp.abs(reduced)) - 1.4e-8
    s2 = s * s
    p = jnp.float32(-0.00737043)
    for c in (0.082145887, -0.59926453, 2.5501640, -5.1677128, 3.1415927):
        p = p * s2 + jnp.float32(c)
    return p * s


def split(value):
    high = value.astype(BF16)
    return high, (value - high.astype(F32)).astype(BF16)


def order_pairs(pair_count, ints, order):
    side = 4
    at_len, at_hgt = lax.axis_index("len"), lax.axis_index("hgt")
    square = (PAIRS, PAIRS)
    down, along = (lax.broadcasted_iota(jnp.int32, square, d) for d in (0, 1))
    slots = lax.broadcasted_iota(jnp.int32, (1, PAIRS), 1)
    slave_face, master_row, master_col, active = (ref[...] for ref in ints)
    live = (slots < pair_count[0, 0]) & (active == 1)
    step_len = master_row // side - at_len
    step_hgt = master_col // side - at_hgt
    column = jnp.where(step_len == 0, OWN, jnp.where(step_len == 1 - 2 * lax.rem(at_len, 2), PARTNER, OTHER))
    row = jnp.where(step_hgt == 0, MID, jnp.where(step_hgt < 0, DOWN, UP))
    spot = (column * 3 + row) * FACES + (master_row % side) * side + master_col % side
    key = jnp.where(live, spot, SPOTS)

    def stand(values):
        return jnp.sum(jnp.where(down == along, values, 0), axis=1, keepdims=True)

    def rank_of(key, key_col):
        before = (key < key_col) | ((key == key_col) & (along < down))
        return jnp.sum(before.astype(jnp.int32), axis=1, keepdims=True)

    def pick(rank, values):
        return jnp.sum(jnp.where(rank == along, values, 0), axis=0, keepdims=True)

    spots = lax.broadcasted_iota(jnp.int32, (PAIRS, META[1]), 1)

    def last_of(key_col):
        has = jnp.sum((key_col == spots).astype(jnp.int32), axis=0, keepdims=True)
        upto = jnp.sum((key_col <= spots).astype(jnp.int32), axis=0, keepdims=True)
        return jnp.where(has > 0, upto - 1, -1)

    key_col = stand(key)
    rank = rank_of(key, key_col)
    face_key = jnp.where(live, slave_face, FACES)
    face_col = stand(face_key)
    face_rank = rank_of(face_key, face_col)
    order[...] = jnp.zeros(META, jnp.int32)
    order[AT_PAIR : AT_PAIR + 1, :PAIRS] = pick(rank, down)
    order[AT_MASTER : AT_MASTER + 1, :PAIRS] = pick(rank, key_col)
    order[AT_SLAVE : AT_SLAVE + 1, :PAIRS] = pick(rank, stand(slave_face))
    order[AT_LAST : AT_LAST + 1, :] = last_of(key_col)
    order[AT_TURN : AT_TURN + 1, :PAIRS] = pick(face_rank, rank)
    order[AT_FACE : AT_FACE + 1, :PAIRS] = pick(face_rank, face_col)
    order[AT_END : AT_END + 1, :] = last_of(face_col)


def kernel(
    pair_count,
    slave_face,
    master_row,
    master_col,
    active,
    coords,
    weights,
    slave_hbm,
    master_hbm,
    out_master,
    out_slave,
    order,
    meta,
    points,
    point_weights,
    window_first,
    window_second,
    slave,
    mortar,
    dual,
    tables,
    first_sq,
    second_sq,
    run,
    mult,
    slave_run,
    send_p,
    recv_p,
    send_o,
    recv_o,
    recv_d,
    send_h,
    recv_h,
    local_sem,
    halo_h_send,
    halo_h_recv,
    halo_p_send,
    halo_p_recv,
    halo_o_send,
    halo_o_recv,
    halo_d_send,
    halo_d_recv,
    halo_f_send,
    halo_f_recv,
    force_l_send,
    force_l_recv,
    force_m_send,
    force_m_recv,
    force_d_send,
    force_d_recv,
    force_h_send,
    force_h_recv,
):
    windows = (window_first, window_second)
    at_len = lax.axis_index("len")
    at_hgt = lax.axis_index("hgt")
    n_len = lax.axis_size("len")
    n_hgt = lax.axis_size("hgt")
    odd = lax.rem(at_len, 2)
    other_len = at_len - 1 + 2 * odd
    partner = (at_len + 1 - 2 * odd, at_hgt)
    other = (lax.rem(other_len + n_len, n_len), at_hgt)
    above = (at_len, lax.rem(at_hgt + 1, n_hgt))
    below = (at_len, lax.rem(at_hgt + n_hgt - 1, n_hgt))
    has_other = (other_len >= 0) & (other_len < n_len)
    has_row = (at_hgt > 0, at_hgt < n_hgt - 1)
    beside = (below, above)
    neighbours = ((partner, None), (other, has_other), (below, has_row[DOWN]), (above, has_row[UP]))

    def when(condition, action):
        if condition is None:
            action()
        else:
            pl.when(condition)(action)

    def remote(src, dst, send_sem, recv_sem, device):
        return pltpu.make_async_remote_copy(
            src_ref=src,
            dst_ref=dst,
            send_sem=send_sem,
            recv_sem=recv_sem,
            device_id=device,
            device_id_type=MESH,
        )

    def faces(g):
        return pl.ds(g * PART, PART)

    def half_of(ref, half, places):
        return ref.at[places, pl.ds(half * ROWS, ROWS)]

    def halo_hgt(half, row, g):
        return remote(
            half_of(master_hbm, half, faces(g)),
            windows[half].at[OWN, 1 - row, faces(g)],
            halo_h_send.at[half, row, g],
            halo_h_recv.at[half, 1 - row, g],
            beside[row],
        )

    def halo_partner(half):
        return remote(
            half_of(master_hbm, half, pl.ds(0, FACES)),
            windows[half].at[PARTNER, MID],
            halo_p_send.at[half],
            halo_p_recv.at[half],
            partner,
        )

    def halo_other(half, g):
        return remote(
            half_of(master_hbm, half, faces(g)),
            windows[half].at[OTHER, MID, faces(g)],
            halo_o_send.at[half, g],
            halo_o_recv.at[half, g],
            other,
        )

    def halo_turn(half, row):
        return remote(
            windows[half].at[OTHER, MID, faces(TURN)],
            windows[half].at[OTHER, 1 - row, faces(TURN)],
            halo_d_send.at[half, row],
            halo_d_recv.at[half, 1 - row],
            beside[row],
        )

    def halo_forward(half, column, row, g):
        return remote(
            windows[half].at[OWN, row, faces(g)],
            windows[half].at[column, row, faces(g)],
            halo_f_send.at[half, column - 1, row, g],
            halo_f_recv.at[half, column - 1, row, g],
            partner if column == PARTNER else other,
        )

    def force_len(half, column, g):
        if column == PARTNER:
            src, dst, device = send_p, recv_p, partner
        else:
            src, dst, device = send_o, recv_o, other
        return remote(
            src.at[half, g, pl.ds(0, 2)],
            dst.at[half, g, pl.ds(0, 2)],
            force_l_send.at[half, column - 1, g],
            force_l_recv.at[half, column - 1, g],
            device,
        )

    def force_mid(half, column, g):
        if column == PARTNER:
            src, dst, device = send_p, recv_p, partner
        else:
            src, dst, device = send_o, recv_o, other
        return remote(
            src.at[half, g, MID],
            dst.at[half, g, MID],
            force_m_send.at[half, column - 1, g],
            force_m_recv.at[half, column - 1, g],
            device,
        )

    def force_turn(half, row):
        return remote(
            send_o.at[half, TURN, row],
            recv_d.at[half, 1 - row],
            force_d_send.at[half, row],
            force_d_recv.at[half, 1 - row],
            beside[row],
        )

    def force_hgt(half, row, g):
        return remote(
            send_h.at[half, row, g],
            recv_h.at[half, 1 - row, g],
            force_h_send.at[half, row, g],
            force_h_recv.at[half, 1 - row, g],
            beside[row],
        )

    def to_other(action):
        pl.when(has_other)(action)

    def to_row(row, action):
        pl.when(has_row[row])(action)

    barrier = pltpu.get_barrier_semaphore()
    for device, there in neighbours:

        def greet(device=device):
            pl.semaphore_signal(barrier, inc=1, device_id=device, device_id_type=MESH)

        when(there, greet)
    loads = [
        pltpu.make_async_copy(coords, points, local_sem.at[0]),
        pltpu.make_async_copy(weights, point_weights, local_sem.at[1]),
        *[
            pltpu.make_async_copy(
                half_of(master_hbm, half, pl.ds(0, FACES)),
                windows[half].at[OWN, MID],
                local_sem.at[2 + half],
            )
            for half in range(HALVES)
        ],
        *[
            pltpu.make_async_copy(
                half_of(slave_hbm, half, pl.ds(0, FACES)), slave.at[half], local_sem.at[4 + half]
            )
            for half in range(HALVES)
        ],
    ]
    for load in loads:
        load.start()
    pl.semaphore_wait(barrier, 1 + sum(there.astype(jnp.int32) for _, there in neighbours[1:]))

    def send_own(half):
        @pl.when(has_other)
        def _():
            for g in (TURN, *range(TURN)):
                halo_other(half, g).start()

        halo_partner(half).start()
        for g in range(CHUNKS):
            for row in (DOWN, UP):
                to_row(row, lambda row=row, g=g: halo_hgt(half, row, g).start())

    send_own(0)
    order_pairs(pair_count, (slave_face, master_row, master_col, active), order)
    publish = pltpu.make_async_copy(order, meta, local_sem.at[6])
    publish.start()
    loads[0].wait()
    loads[1].wait()

    modes = lax.broadcasted_iota(jnp.int32, (ORDER, NODES), 0).astype(F32)
    row_ids = lax.broadcasted_iota(jnp.int32, (NODES, NODES), 0)
    col_ids = lax.broadcasted_iota(jnp.int32, (NODES, NODES), 1)

    def build_tables(first_pair):
        def one(i, _):
            place = points[first_pair + i]
            weight = point_weights[pl.ds(first_pair + i, 1), :]
            sx, sy, mx, my = (cos_pi(modes * place[k : k + 1]) for k in range(4))
            rows = pl.ds(pl.multiple_of((first_pair + i) * ORDER, ORDER), ORDER)
            tables[i, 0] = sx
            tables[i, 1] = sy
            tables[i, 2] = mx * weight
            tables[i, 3] = my
            first_sq[rows, :] = sx * sx * weight
            second_sq[rows, :] = sy * sy
            return 0

        lax.fori_loop(0, GROUP, one, 0)

    def build_dual():
        same_pair = row_ids // ORDER == col_ids // ORDER
        same_node = row_ids % ORDER == col_ids // ORDER
        spread = jnp.where(row_ids % ORDER == col_ids % ORDER, 1.0, 0.0).astype(BF16)
        spread = jnp.concatenate([spread, spread], axis=0)
        for k in range(PAIRS // SQUARES):
            rows = pl.ds(k * SQUARES * ORDER, SQUARES * ORDER)
            high, low = split(first_sq[rows, :])
            left = jnp.concatenate([high, low, high], axis=1)
            high, low = split(second_sq[rows, :])
            right = jnp.concatenate([high, high, low], axis=1)
            sums = lax.dot_general(left, right, NT, preferred_element_type=F32)
            high, low = split(jnp.where(same_pair, sums, 0.0))
            wide = jnp.dot(
                jnp.concatenate([high, low], axis=1), spread, preferred_element_type=F32
            )
            wide = jnp.where(same_node, wide, 0.0)
            dual[k * SQUARES : (k + 1) * SQUARES, :] = jnp.sum(wide.reshape(SQUARES, ORDER, NODES), axis=1)

    def table_of(i, k):
        first, second = tables[i, k], tables[i, k + 1]
        return (first[:, None, :] * second[None, :, :]).reshape(NODES, NODES)

    def build_mortar(first_pair):
        def some(step, _):
            for u in range(LOCK_A):
                i = step * LOCK_A + u
                slave_high, slave_low = split(table_of(i, 0))
                master_high, master_low = split(table_of(i, 2))
                left = jnp.concatenate([slave_high, slave_low, slave_high], axis=1)
                right = jnp.concatenate([master_high, master_high, master_low], axis=1)
                product = lax.dot_general(left, right, NT, preferred_element_type=F32)
                mortar[first_pair + i] = product.astype(BF16)
            return 0

        lax.fori_loop(0, GROUP // LOCK_A, some, 0)

    def relay(half, g):
        @pl.when((g == 0) & has_other)
        def _():
            halo_other(half, TURN).wait_recv()
            for row in (DOWN, UP):
                to_row(row, lambda row=row: halo_turn(half, row).start())

        for row in (DOWN, UP):

            def pass_on(row=row):
                halo_hgt(half, 1 - row, g).wait_recv()
                pl.when(has_other & (g != TURN))(lambda: halo_forward(half, OTHER, row, g).start())
                halo_forward(half, PARTNER, row, g).start()

            to_row(row, pass_on)

    def prepare(g, _):
        build_tables(g * GROUP)
        build_mortar(g * GROUP)
        for at, chunk in ((1, 0), (4, 2)):
            pl.when((g == at) | (g == at + 1))(lambda: relay(0, chunk + g - at))
        pl.when(g == 4)(lambda: send_own(1))
        return 0

    lax.fori_loop(0, PAIRS // GROUP, prepare, 0)
    build_dual()

    @pl.when(jnp.logical_not(has_other))
    def _():
        recv_o[...] = jnp.zeros(recv_o.shape, BF16)

    for row in (DOWN, UP):

        @pl.when(jnp.logical_not(has_row[row]))
        def _(row=row):
            for half in range(HALVES):
                recv_h[half, row] = jnp.zeros(recv_h.shape[2:], BF16)
                recv_d[half, row] = jnp.zeros(recv_d.shape[2:], BF16)

    publish.wait()
    for load in loads[2:]:
        load.wait()

    def all_arrived(half):
        halo_partner(half).wait_recv()

        def arrived(g, _):
            pl.when(has_other & (g != TURN))(lambda: halo_other(half, g).wait_recv())
            for row in (DOWN, UP):

                def rest(row=row):
                    halo_forward(half, PARTNER, row, g).wait_recv()
                    pl.when(has_other & (g != TURN))(lambda: halo_forward(half, OTHER, row, g).wait_recv())
                    pl.when(has_other & (g == TURN))(lambda: halo_turn(half, 1 - row).wait_recv())

                to_row(row, rest)
            return 0

        lax.fori_loop(0, CHUNKS, arrived, 0)

    def contact(half, step):
        slots = [step * LOCK_B + u for u in range(LOCK_B)]
        pairs = [meta[AT_PAIR, t] for t in slots]
        keys = [meta[AT_MASTER, t] for t in slots]
        mortars = [mortar[p] for p in pairs]
        projected = []
        for key, matrix in zip(keys, mortars):
            spot = jnp.where(key < SPOTS, key, MID * FACES)
            block = spot // FACES
            master = windows[half][block // 3, block % 3, spot % FACES]
            projected.append(lax.dot_general(master, matrix, NT, preferred_element_type=F32))
        multipliers = []
        for t, p, key, part in zip(slots, pairs, keys, projected):
            diag = dual[pl.ds(p, 1), :]
            gap = slave[half, meta[AT_SLAVE, t]].astype(F32) * diag - part
            multipliers.append(jnp.where(key < SPOTS, gap * (1.0 / diag), 0.0))
        pushes = [
            jnp.dot(m.astype(BF16), matrix, preferred_element_type=F32)
            for m, matrix in zip(multipliers, mortars)
        ]
        for t, m in zip(slots, multipliers):
            mult[half, t] = m
        total = run[half, jnp.maximum(slots[0] - 1, 0)]
        last = meta[AT_MASTER, jnp.maximum(slots[0] - 1, 0)]
        for t, key, push in zip(slots, keys, pushes):
            total = jnp.where(key == last, total, 0.0) + push
            run[half, t] = total
            last = key

    def force(half, column, row, face):
        last = meta[AT_LAST, (column * 3 + row) * FACES + face]
        return jnp.where(last >= 0, run[half, jnp.maximum(last, 0)], 0.0)

    def fill(half, column, g, rows):
        send = send_p if column == PARTNER else send_o
        for row in rows:
            for i in range(PART):
                send[half, g, row, i] = force(half, column, row, g * PART + i).astype(send.dtype)

    def send_all(half):
        def side(k, _):
            g = lax.rem(k + TURN, CHUNKS)
            fill(half, OTHER, g, (DOWN, UP))

            @pl.when(g == TURN)
            def _():
                for row in (DOWN, UP):
                    to_row(row, lambda row=row: force_turn(half, row).start())

            pl.when(has_other & (g != TURN))(lambda: force_len(half, OTHER, g).start())
            return 0

        def partner_side(k, _):
            g = lax.rem(k + TURN, CHUNKS)
            fill(half, PARTNER, g, (DOWN, UP))
            force_len(half, PARTNER, g).start()
            return 0

        def middle(g, _):
            fill(half, OTHER, g, (MID,))
            to_other(lambda: force_mid(half, OTHER, g).start())
            return 0

        def partner_middle(g, _):
            fill(half, PARTNER, g, (MID,))
            force_mid(half, PARTNER, g).start()
            return 0

        lax.fori_loop(0, CHUNKS, side, 0)
        lax.fori_loop(0, CHUNKS, partner_side, 0)
        lax.fori_loop(0, TURN, middle, 0)
        lax.fori_loop(0, CHUNKS, partner_middle, 0)

    def add_slaves(half):
        slave_run[0] = jnp.zeros((ROWS, NODES), F32)

        def some(step, _):
            first = step * LOCK_S
            total = slave_run[jnp.maximum(first - 1, 0)]
            last = meta[AT_FACE, jnp.maximum(first - 1, 0)]
            for u in range(LOCK_S):
                face = meta[AT_FACE, first + u]
                total = jnp.where(face == last, total, 0.0) + mult[half, meta[AT_TURN, first + u]]
                slave_run[first + u] = total
                last = face
            return 0

        lax.fori_loop(0, PAIRS // LOCK_S, some, 0)

        def one(face, _):
            last = meta[AT_END, face]
            total = jnp.where(last >= 0, slave_run[jnp.maximum(last, 0)], 0.0)
            out_slave[face, half * ROWS : (half + 1) * ROWS, :] = total
            return 0

        lax.fori_loop(0, FACES, one, 0)

    def send_heights(half, k):
        g = lax.rem(k + TURN, CHUNKS)
        force_len(half, PARTNER, g).wait_recv()

        def own(row, i):
            return force(half, OWN, row, g * PART + i) + recv_p[half, g, row, i]

        @pl.when(g == TURN)
        def _():
            for row in (DOWN, UP):
                for i in range(PART):
                    send_h[half, row, g, i] = own(row, i).astype(BF16)

        @pl.when(g != TURN)
        def _():
            to_other(lambda: force_len(half, OTHER, g).wait_recv())
            for row in (DOWN, UP):
                for i in range(PART):
                    total = own(row, i) + recv_o[half, g, row, i].astype(F32)
                    send_h[half, row, g, i] = total.astype(BF16)

        for row in (DOWN, UP):
            to_row(row, lambda row=row: force_hgt(half, row, g).start())

    def send_turned(half):
        for row in (DOWN, UP):
            to_row(row, lambda row=row: force_turn(half, 1 - row).wait_recv())
        for i in range(PART):
            total = force(half, OTHER, MID, TURN * PART + i)
            for row in (DOWN, UP):
                total = total + recv_d[half, row, i].astype(F32)
            send_o[half, TURN, MID, i] = total.astype(BF16)
        to_other(lambda: force_mid(half, OTHER, TURN).start())

    def finish(half, g):
        force_mid(half, PARTNER, g).wait_recv()
        to_other(lambda: force_mid(half, OTHER, g).wait_recv())
        for row in (DOWN, UP):
            to_row(row, lambda row=row: force_hgt(half, 1 - row, g).wait_recv())
        for i in range(PART):
            total = force(half, OWN, MID, g * PART + i)
            total = total + recv_p[half, g, MID, i] + recv_o[half, g, MID, i].astype(F32)
            for row in (DOWN, UP):
                total = total + recv_h[half, row, g, i].astype(F32)
            out_master[g * PART + i, half * ROWS : (half + 1) * ROWS, :] = total

    for half in range(HALVES):
        run[half, 0] = jnp.zeros((ROWS, NODES), F32)

    all_arrived(0)
    relay(1, 0)

    def first_half(k, _):
        contact(0, k)
        pl.when(k % 2 == 0)(lambda: relay(1, k // 2 + 1))
        return 0

    lax.fori_loop(0, PAIRS // LOCK_B, first_half, 0)
    send_all(0)
    relay(1, 3)

    all_arrived(1)

    def second_half(k, _):
        contact(1, k)
        send_heights(0, k)
        return 0

    lax.fori_loop(0, PAIRS // LOCK_B, second_half, 0)
    send_turned(0)
    send_all(1)

    def last_sums(k, _):
        send_heights(1, k)
        for half in range(HALVES):
            pl.when(k == half)(lambda half=half: add_slaves(half))
        pl.when(k == 2)(lambda: send_turned(1))
        return 0

    lax.fori_loop(0, CHUNKS, last_sums, 0)

    for half in range(HALVES):

        def last_faces(g, _, half=half):
            finish(half, g)
            return 0

        lax.fori_loop(0, CHUNKS, last_faces, 0)

    for half in range(HALVES):
        halo_partner(half).wait_send()
        for row in (DOWN, UP):
            to_row(row, lambda row=row, half=half: force_turn(half, row).wait_send())
            pl.when(has_row[row] & has_other)(
                lambda row=row, half=half: halo_turn(half, row).wait_send()
            )

        def sent(g, _, half=half):
            to_other(lambda: halo_other(half, g).wait_send())
            force_len(half, PARTNER, g).wait_send()
            force_mid(half, PARTNER, g).wait_send()
            to_other(lambda: force_mid(half, OTHER, g).wait_send())
            pl.when(has_other & (g != TURN))(lambda: force_len(half, OTHER, g).wait_send())
            for row in (DOWN, UP):

                def rest(row=row):
                    halo_hgt(half, row, g).wait_send()
                    force_hgt(half, row, g).wait_send()
                    halo_forward(half, PARTNER, row, g).wait_send()
                    pl.when(has_other & (g != TURN))(lambda: halo_forward(half, OTHER, row, g).wait_send())

                to_row(row, rest)
            return 0

        lax.fori_loop(0, CHUNKS, sent, 0)


def store(master_in, slave_in, master_out, slave_out, sem):
    copies = []
    for k in range(CHUNKS):
        at = pl.ds(k * PART, PART)
        copies.append(pltpu.make_async_copy(master_in.at[at], master_out.at[at], sem.at[0, k]))
        copies.append(pltpu.make_async_copy(slave_in.at[at], slave_out.at[at], sem.at[1, k]))
    for copy in copies:
        copy.start()
    for copy in copies:
        copy.wait()


def body(
    slave_disp,
    master_disp,
    quad_coords,
    quad_weights,
    pair_count,
    slave_face,
    master_row,
    master_col,
    active,
):
    face = (CHANNELS, NODES)
    dma = pltpu.SemaphoreType.DMA
    out = jax.ShapeDtypeStruct((FACES, *face), F32)
    held = pltpu.VMEM((FACES, *face), F32)
    vmem = pl.BlockSpec(memory_space=pltpu.VMEM)
    hbm = pl.BlockSpec(memory_space=pl.ANY)
    slots = (1, PAIRS)
    part = (ROWS, NODES)
    results = pl.pallas_call(
        kernel,
        out_shape=(held, held),
        in_specs=[pl.BlockSpec(memory_space=pltpu.SMEM), *[vmem] * 4, *[hbm] * 4],
        out_specs=(vmem, vmem),
        scratch_shapes=[
            pltpu.VMEM(META, jnp.int32),
            pltpu.SMEM(META, jnp.int32),
            pltpu.VMEM((PAIRS, 4, NODES), F32),
            pltpu.VMEM((PAIRS, NODES), F32),
            *[pltpu.VMEM((3, 3, FACES, *part), BF16)] * HALVES,
            pltpu.VMEM((HALVES, FACES, *part), BF16),
            pltpu.VMEM((PAIRS, NODES, NODES), BF16),
            pltpu.VMEM((PAIRS, NODES), F32),
            pltpu.VMEM((GROUP, 4, ORDER, NODES), F32),
            pltpu.VMEM((PAIRS * ORDER, NODES), F32),
            pltpu.VMEM((PAIRS * ORDER, NODES), F32),
            pltpu.VMEM((HALVES, PAIRS, *part), F32),
            pltpu.VMEM((HALVES, PAIRS, *part), F32),
            pltpu.VMEM((PAIRS, *part), F32),
            pltpu.VMEM((HALVES, CHUNKS, 3, PART, *part), F32),
            pltpu.VMEM((HALVES, CHUNKS, 3, PART, *part), F32),
            pltpu.VMEM((HALVES, CHUNKS, 3, PART, *part), BF16),
            pltpu.VMEM((HALVES, CHUNKS, 3, PART, *part), BF16),
            pltpu.VMEM((HALVES, 2, PART, *part), BF16),
            pltpu.VMEM((HALVES, 2, CHUNKS, PART, *part), BF16),
            pltpu.VMEM((HALVES, 2, CHUNKS, PART, *part), BF16),
            dma((7,)),
            *[dma((HALVES, 2, CHUNKS))] * 2,
            *[dma((HALVES,))] * 2,
            *[dma((HALVES, CHUNKS))] * 2,
            *[dma((HALVES, 2))] * 2,
            *[dma((HALVES, 2, 2, CHUNKS))] * 2,
            *[dma((HALVES, 2, CHUNKS))] * 2,
            *[dma((HALVES, 2, CHUNKS))] * 2,
            *[dma((HALVES, 2))] * 2,
            *[dma((HALVES, 2, CHUNKS))] * 2,
        ],
        compiler_params=pltpu.CompilerParams(
            collective_id=0, has_side_effects=True, vmem_limit_bytes=57 * 2**20
        ),
        name="contact",
    )(
        pair_count,
        slave_face.reshape(slots),
        master_row.reshape(slots),
        master_col.reshape(slots),
        active.reshape(slots),
        quad_coords.reshape(PAIRS, 4, NODES),
        quad_weights.reshape(PAIRS, NODES),
        slave_disp.reshape(FACES, *face),
        master_disp.reshape(FACES, *face),
    )
    results = [pltpu.with_memory_space_constraint(r, pltpu.VMEM) for r in results]
    master_force, slave_sum = pl.pallas_call(
        store,
        out_shape=(out, out),
        in_specs=[vmem, vmem],
        out_specs=(hbm, hbm),
        scratch_shapes=[dma((2, CHUNKS))],
        compiler_params=pltpu.CompilerParams(vmem_limit_bytes=2**20),
        name="store",
    )(*results)
    return (
        master_force.reshape(4, 4, *face),
        slave_sum.reshape(4, 4, *face),
    )


def solution(mesh):
    in_specs = (
        P("len", "hgt", None, None),
        P("len", "hgt", None, None),
        P("len", "hgt", None, None, None),
        P("len", "hgt", None, None),
        P("len", "hgt"),
        P("len", "hgt", None),
        P("len", "hgt", None),
        P("len", "hgt", None),
        P("len", "hgt", None),
    )
    out_specs = (P("len", "hgt", None, None), P("len", "hgt", None, None))
    return jax.shard_map(body, mesh=mesh, in_specs=in_specs, out_specs=out_specs, check_vma=False)
```
